256 devices in a mesh: dp: 8 (over z_hi, x), expert: 32 (over z_lo, y, core).
Axes of the slice: x: 4, y: 4, z: 8 (z_hi: 2, z_lo: 4; z = z_hi * 4 + z_lo), core: 2. Of those that a mesh axis runs over, the one named last changes fastest.
Arguments:
- tokens: bfloat16 [32768, 1792], P(('dp', 'expert')), may hold values from -6 to 6
- routes: int32 [32768, 4], P(('dp', 'expert')), may hold values from 0 to 31, all different within a row; in each aligned block of 128 rows (0 to 127, 128 to 255, ...) at most 32 rows name the same one
- route_weight: float32 [32768, 4], P(('dp', 'expert')), may hold values from 0.1 to 1
- w_in: float32 [32, 2, 1792, 1280], P('expert', None, 'dp'), may hold values from -0.125 to 0.125
- m_in: float32 [32, 2, 1792, 1280], P('expert', None, 'dp'), may hold values from -6 to 6
- v_in: float32 [32, 2, 1792, 1280], P('expert', None, 'dp'), may hold values from 0.5 to 20
- g_in: bfloat16 [32, 2, 1792, 1280], P('expert', None, 'dp'), may hold values from -30 to 30
- w_out: float32 [32, 1280, 1792], P('expert', 'dp'), may hold values from -0.15625 to 0.15625
- m_out: float32 [32, 1280, 1792], P('expert', 'dp'), may hold values from -6 to 6
- v_out: float32 [32, 1280, 1792], P('expert', 'dp'), may hold values from 0.5 to 20
- g_out: bfloat16 [32, 1280, 1792], P('expert', 'dp'), may hold values from -30 to 30
Outputs:
- mixed: bfloat16 [32768, 1792], P(('dp', 'expert'))
The draws below stay inside these ranges and needn't reach their ends.
Inputs may be any that keep to these rules, and one draw needn't show every extreme that they name: `routes`: A token's 4 experts differ. Within the rows of one device (aligned blocks of 128 tokens) each expert is named at most 32 times, a bound that some block reaches.
All inputs are finite; a program needn't handle non-finite values.
Results may differ from the reference program's by a relative error of at most 0.008.
Values may be sent and summed in bfloat16 or wider, within the bound.
A program may use at most 128 MiB of HBM per device.

```python
import math
import jax
import jax.numpy as jnp
import numpy as np
from jax import lax

D = 1792
HIDDEN_SIZE = 1280
TOPW = 4
TOK_DEV = 128
EXPERTS = 32
CAP = 32
TOKENS = 32768
N_DP = 8
N_EXPERT = 32


def block_scale(key, extent, shards, smallest, high):
    loudness = 1.0
    for dim, blocks in shards:
        steps = jax.random.uniform(jax.random.fold_in(jax.random.fold_in(key, 6), dim), (blocks,), jnp.float32, smallest / len(shards), high / len(shards))
        loudness = loudness * jnp.repeat(jnp.exp(steps), extent[dim] // blocks).reshape((-1,) + (1,) * (len(extent) - 1 - dim))
    return loudness


def shared_out(rng, own, number, rows, number_of, top, reach, slope):
    sequence = jax.random.permutation(rng, number_of)
    packed, ordinary = shares(number_of, rows * top, reach, slope, True), shares(number_of, rows * top, reach, slope, False)
    places = jnp.arange(number_of)

    def named(tallies, rotation):
        used = int((tallies > 0).sum())
        fixed = max(1, used // 4)
        passed = fixed + (places - fixed + rotation * (used - fixed)) % max(1, number_of - fixed)
        return jnp.zeros((number_of,), jnp.int32).at[sequence[jnp.where(places < fixed, places, passed)]].set(jnp.asarray(tallies, jnp.int32))

    tallies = jnp.where(number % 4 == 0, named(packed, number // 4), named(ordinary, number - number // 4 - 1))
    mixed = jax.random.permutation(jax.random.fold_in(own, 3), number_of)
    giver, receiver = mixed[0:number_of // 2 * 2:2], mixed[1:number_of // 2 * 2:2]
    slack = jnp.minimum(tallies[giver] - 1, reach - tallies[receiver]) // 2
    slack = jnp.where((giver == sequence[0]) | (receiver == sequence[0]) | (tallies[receiver] == 0), 0, jnp.maximum(slack, 0))
    passed = jax.random.randint(jax.random.fold_in(own, 4), (number_of // 2,), 0, 1 << 20) % (slack + 1)
    tallies = tallies.at[giver].add(-passed).at[receiver].add(passed)
    members = jnp.searchsorted(jnp.cumsum(tallies), jnp.arange(rows * top), side="right").astype(jnp.int32)
    grid = members.reshape(top, rows).T
    grid = grid[jax.random.permutation(jax.random.fold_in(own, 1), rows)]
    rotation = jax.random.randint(jax.random.fold_in(own, 2), (rows, 1), 0, top)
    return jnp.take_along_axis(grid, (jnp.arange(top)[None, :] + rotation) % top, axis=1)


def shares(count, total, most, slope, full):
    loads = [(1 << 20) // math.isqrt(rank ** slope) + 1 for rank in range(1, count + 1)]
    largest = most if full else min(most, max(-(-total // count), total * loads[0] // sum(loads)))
    least = 1 if total - largest >= count - 1 else 0
    counts, rest = [largest] + [least] * (count - 1), total - largest - least * (count - 1)
    while rest > 0:
        free = [i for i in range(1, count) if counts[i] < largest] or [i for i in range(1, count) if counts[i] < most]
        pool, budget = sum([loads[i] for i in free]), rest
        for i in free:
            more = min(most - counts[i], max(1, budget * loads[i] // pool), rest)
            counts[i] = counts[i] + more
            rest = rest - more
    return np.array(counts)


def gaussian(own_key, shape, spread, reach, cuts=(), kind=jnp.bfloat16):
    gain = block_scale(own_key, shape, cuts, -0.22, 0.18) if cuts else 1.0
    values = jax.random.normal(own_key, shape, jnp.float32) * spread * gain
    return jnp.minimum(jnp.maximum(values, -reach), reach).astype(kind)


def setup_inputs(seed: int = 0) -> dict:
    arg_keys = jax.random.split(jax.random.key(seed), 12)
    tokens = gaussian(arg_keys[0], (TOKENS, D), 1.0, 6.0, ((0, 256),))
    routes_keys = jax.random.split(jax.random.fold_in(arg_keys[1], 1), TOKENS // TOK_DEV)
    routes_turns = jax.random.permutation(jax.random.fold_in(arg_keys[1], 3), TOKENS // TOK_DEV)
    routes = jax.vmap(lambda own, number: shared_out(jax.random.fold_in(arg_keys[1], 2), own, number, TOK_DEV, EXPERTS, TOPW, CAP, 2))(routes_keys, routes_turns).reshape((TOKENS, TOPW))
    route_weight = jnp.clip(0.1 + 0.9 * jax.random.uniform(arg_keys[2], (TOKENS, TOPW), jnp.float32) ** block_scale(arg_keys[2], (TOKENS, TOPW), ((0, 256),), -0.2, 0.2), 0.1, 1.0)
    w_in = gaussian(arg_keys[3], (EXPERTS, 2, D, HIDDEN_SIZE), D ** -0.5, 0.125, ((0, 32), (2, 8)), jnp.float32)
    m_in = gaussian(arg_keys[4], (EXPERTS, 2, D, HIDDEN_SIZE), 1.0, 6.0, ((0, 32), (2, 8)), jnp.float32)
    v_in = jnp.clip(jnp.exp(math.log(20.0) - 3.6888795 * jax.random.uniform(arg_keys[5], (EXPERTS, 2, D, HIDDEN_SIZE), jnp.float32) ** block_scale(arg_keys[5], (EXPERTS, 2, D, HIDDEN_SIZE), ((0, 32), (2, 8)), -0.2, 0.2)), 0.5, 20.0)
    g_in = gaussian(arg_keys[6], (EXPERTS, 2, D, HIDDEN_SIZE), 5.0, 30.0, ((0, 32), (2, 8)))
    w_out = gaussian(arg_keys[7], (EXPERTS, HIDDEN_SIZE, D), HIDDEN_SIZE ** -0.5, 0.15625, ((0, 32), (1, 8)), jnp.float32)
    m_out = gaussian(arg_keys[8], (EXPERTS, HIDDEN_SIZE, D), 1.0, 6.0, ((0, 32), (1, 8)), jnp.float32)
    v_out = jnp.clip(jnp.exp(math.log(20.0) - 3.6888795 * jax.random.uniform(arg_keys[9], (EXPERTS, HIDDEN_SIZE, D), jnp.float32) ** block_scale(arg_keys[9], (EXPERTS, HIDDEN_SIZE, D), ((0, 32), (1, 8)), -0.2, 0.2)), 0.5, 20.0)
    g_out = gaussian(arg_keys[10], (EXPERTS, HIDDEN_SIZE, D), 5.0, 30.0, ((0, 32), (1, 8)))
    return dict(tokens=tokens, routes=routes, route_weight=route_weight, w_in=w_in, m_in=m_in, v_in=v_in, g_in=g_in, w_out=w_out, m_out=m_out, v_out=v_out, g_out=g_out)


beta_one = 0.9
beta_two = 0.95
corr_one = 0.99997343860111
corr_two = 0.99407947077967
adam_eps = 1e-08
learn_rate = 0.01
weight_decay = 0.1

def adamw(master, moment, second, gradient):
    grad_value = gradient.astype(jnp.float32)
    moment_new = beta_one * moment + (1.0 - beta_one) * grad_value
    second_new = beta_two * second + (1.0 - beta_two) * grad_value * grad_value
    update = moment_new / corr_one / (jnp.sqrt(second_new / corr_two) + adam_eps)
    return (master - learn_rate * (update + weight_decay * master)).astype(jnp.bfloat16)

def reference(tokens, routes, route_weight, w_in, m_in, v_in, g_in, w_out, m_out, v_out, g_out):
    limit = N_DP * N_EXPERT * CAP
    entry_count = TOKENS * TOPW
    flat_routes = routes.reshape(-1)
    owners = jnp.arange(entry_count, dtype=jnp.int32) // TOPW
    flat_weight = route_weight.reshape(-1)
    positions = jnp.arange(limit, dtype=jnp.int32)

    def one_expert(totals, inputs):
        expert_id, master_in, moment_in, second_in, grad_in, master_out, moment_out, second_out, grad_out = inputs
        gate_up = adamw(master_in, moment_in, second_in, grad_in)
        down_proj = adamw(master_out, moment_out, second_out, grad_out)
        hits = flat_routes == expert_id
        picks = jnp.nonzero(hits, size=limit, fill_value=0)[0].astype(jnp.int32)
        valid = (positions < jnp.sum(hits.astype(jnp.int32))).astype(jnp.float32)
        token_ids = jnp.take(owners, picks).astype(jnp.int32)
        block_rows = jnp.take(tokens, token_ids, axis=0)
        gate_pre = jnp.dot(block_rows, gate_up[0], preferred_element_type=jnp.float32)
        up_pre = jnp.dot(block_rows, gate_up[1], preferred_element_type=jnp.float32)
        hidden = (jax.nn.silu(gate_pre) * up_pre).astype(jnp.bfloat16)
        results = jnp.dot(hidden, down_proj, preferred_element_type=jnp.float32).astype(jnp.bfloat16)
        scaled = results.astype(jnp.float32) * (jnp.take(flat_weight, picks) * valid)[:, None]
        return (totals.at[token_ids].add(scaled), None)
    scanned = lax.scan(one_expert, jnp.zeros((TOKENS, D), jnp.float32), (jnp.arange(EXPERTS, dtype=jnp.int32), w_in, m_in, v_in, g_in, w_out, m_out, v_out, g_out))
    return scanned[0].astype(jnp.bfloat16)
```

```python
import functools

import jax
import jax.numpy as jnp
from jax import lax
from jax.experimental import pallas as pl
from jax.experimental.pallas import tpu as pltpu
from jax.sharding import PartitionSpec as P

MESH = pl.DeviceIdType.MESH
beta_one = 0.9
beta_two = 0.95
corr_one = 0.99997343860111
corr_two = 0.99407947077967
adam_eps = 1e-08
learn_rate = 0.01
weight_decay = 0.1
XN, YN, ZN = 4, 4, 4
HALVES = 6


def adamw(master, moment, second, gradient):
    grad_value = gradient.astype(jnp.float32)
    moment_new = beta_one * moment + (1.0 - beta_one) * grad_value
    second_new = beta_two * second + (1.0 - beta_two) * grad_value * grad_value
    update = moment_new / corr_one / (jnp.sqrt(second_new / corr_two) + adam_eps)
    return (master - learn_rate * (update + weight_decay * master)).astype(jnp.bfloat16)


def gather_kernel(
    tok, w_in, m_in, v_in, g_in, w_out, m_out, v_out, g_out,
    gu_all, dn_all, tok_all,
    wi, mi, vi, gi, wo, mo, vo, go, gu_own, dn_own,
    load_sem, keep_sem, w_send, w_recv, t_send, t_recv,
):
    d, e = lax.axis_index("dp"), lax.axis_index("expert")
    zh, x = d // XN, d % XN
    z, y, c = e // (2 * YN), e // 2 % YN, e % 2
    at_dp = lambda h, i: h * XN + lax.rem(i + XN, XN)
    right, left, far = at_dp(zh, x + 1), at_dp(zh, x - 1), at_dp(zh, x + 2)
    mirror = at_dp(1 - zh, x)
    p_right, p_left, p_far = at_dp(1 - zh, x + 1), at_dp(1 - zh, x - 1), at_dp(1 - zh, x + 2)
    at_ex = lambda zz, yy, cc: lax.rem(zz + ZN, ZN) * (2 * YN) + lax.rem(yy + YN, YN) * 2 + cc

    half_in, half_out = w_in.shape[0] // 4, w_out.shape[0] // 2
    loads = []
    for h in range(HALVES):
        pairs = (
            ((w_in, wi), (m_in, mi), (v_in, vi), (g_in, gi))
            if h < 4
            else ((w_out, wo), (m_out, mo), (v_out, vo), (g_out, go))
        )
        rows = pl.ds(h * half_in, half_in) if h < 4 else pl.ds((h - 4) * half_out, half_out)
        loads.append(
            [pltpu.make_async_copy(a.at[rows], b.at[rows], load_sem.at[h, i]) for i, (a, b) in enumerate(pairs)]
        )
        for cp in loads[h]:
            cp.start()

    partners = [{"dp": right, "expert": e}, {"dp": left, "expert": e}, {"dp": mirror, "expert": e}]
    partners += [{"dp": d, "expert": at_ex(z + k, y, c)} for k in range(1, ZN)]
    partners += [{"dp": d, "expert": at_ex(z, y + k, c)} for k in range(1, YN)]
    partners += [{"dp": d, "expert": at_ex(z, y, 1 - c)}]
    barrier = pltpu.get_barrier_semaphore()
    for p in partners:
        pl.semaphore_signal(barrier, inc=1, device_id=p, device_id_type=MESH)
    pl.semaphore_wait(barrier, len(partners))

    sent = []

    def tok_copy(slot, target, op, src=None):
        return pltpu.make_async_remote_copy(
            src_ref=tok_all.at[slot] if src is None else src, dst_ref=tok_all.at[slot],
            send_sem=t_send.at[op], recv_sem=t_recv.at[op],
            device_id={"dp": d, "expert": target}, device_id_type=MESH,
        )

    TZ = lambda k: k - 1
    TY = lambda j, k: 3 + j * 3 + k - 1
    TS = lambda j, k: 15 + j * 4 + k

    def tok_send(slot, target, op, src=None):
        cp = tok_copy(slot, target, op, src)
        cp.start()
        sent.append(cp)

    def tok_wait(slot, op):
        tok_copy(slot, at_ex(z, y, 1 - c), op).wait_recv()

    own_tok = pltpu.make_async_copy(tok, tok_all.at[e], keep_sem.at[0])
    own_tok.start()
    for k in (1, 3, 2):
        tok_send(e, at_ex(z + k, y, c), TZ(k), tok)
    for k in (1, 3, 2):
        tok_send(e, at_ex(z, y + k, c), TY(0, k), tok)
    tok_send(e, at_ex(z, y, 1 - c), TS(0, 0), tok)

    def tok_z(j):
        slot = at_ex(z - j, y, c)
        tok_wait(slot, TZ(j))
        for k in (1, 3, 2):
            tok_send(slot, at_ex(z, y + k, c), TY(j, k))
        tok_send(slot, at_ex(z, y, 1 - c), TS(j, 0))

    def tok_y(j, k):
        slot = at_ex(z - j, y - k, c)
        tok_wait(slot, TY(j, k))
        tok_send(slot, at_ex(z, y, 1 - c), TS(j, k))

    def slot_of(h, owner):
        if h < 4:
            return gu_all.at[h // 2, owner, pl.ds(h % 2 * half_in, half_in)]
        return dn_all.at[owner, pl.ds((h - 4) * half_out, half_out)]

    def own_of(h):
        return gu_own.at[pl.ds(h * half_in, half_in)] if h < 4 else dn_own.at[pl.ds((h - 4) * half_out, half_out)]

    def w_copy(h, owner, target, kind, src=None):
        op = kind * HALVES + h
        return pltpu.make_async_remote_copy(
            src_ref=slot_of(h, owner) if src is None else src, dst_ref=slot_of(h, owner),
            send_sem=w_send.at[op], recv_sem=w_recv.at[op],
            device_id={"dp": target, "expert": e}, device_id_type=MESH,
        )

    R_OWN, L_OWN, MIR, F_OWN, R_P, L_P, F_P = range(7)

    def w_send_to(h, owner, target, kind, src=None):
        cp = w_copy(h, owner, target, kind, src)
        cp.start()
        sent.append(cp)

    def w_wait(h, owner, kind):
        w_copy(h, owner, right, kind).wait_recv()

    keeps = [own_tok]
    for h in range(HALVES):
        for cp in loads[h]:
            cp.wait()
        a, b, v, g, out, rows, first = (
            (wi, mi, vi, gi, gu_own, half_in, h * half_in)
            if h < 4
            else (wo, mo, vo, go, dn_own, half_out, (h - 4) * half_out)
        )

        def step(i, _, a=a, b=b, v=v, g=g, out=out, first=first):
            at = pl.ds(pl.multiple_of(first + i * 16, 16), 16)
            out[at, :] = adamw(a[at, :], b[at, :], v[at, :], g[at, :])
            return 0

        lax.fori_loop(0, rows // 16, step, 0)
        w_send_to(h, d, mirror, MIR, own_of(h))
        w_send_to(h, d, right, R_OWN, own_of(h))
        w_send_to(h, d, left, L_OWN, own_of(h))
        keep = pltpu.make_async_copy(own_of(h), slot_of(h, d), keep_sem.at[1 + h])
        keep.start()
        keeps.append(keep)

    def fwd_own(h):
        w_wait(h, left, R_OWN)
        w_wait(h, right, L_OWN)
        if h % 2 == 0:
            w_send_to(h, left, right, F_OWN)
        else:
            w_send_to(h, right, left, F_OWN)

    def from_mirror(h):
        w_wait(h, mirror, MIR)
        w_send_to(h, mirror, right, R_P)
        w_send_to(h, mirror, left, L_P)

    def fwd_mirror(h):
        w_wait(h, p_left, R_P)
        w_wait(h, p_right, L_P)
        if h % 2 == 0:
            w_send_to(h, p_left, right, F_P)
        else:
            w_send_to(h, p_right, left, F_P)

    fwd_own(0)
    tok_z(1)
    fwd_own(1)
    tok_z(3)
    from_mirror(0)
    fwd_own(2)
    tok_z(2)
    fwd_own(3)
    from_mirror(1)
    fwd_own(4)
    from_mirror(2)
    fwd_own(5)
    for k in (1, 3, 2):
        tok_y(0, k)
    fwd_mirror(0)
    from_mirror(3)
    fwd_mirror(1)
    for k in (1, 3, 2):
        tok_y(1, k)
    from_mirror(4)
    fwd_mirror(2)
    for k in (1, 3, 2):
        tok_y(3, k)
    from_mirror(5)
    fwd_mirror(3)
    for k in (1, 3, 2):
        tok_y(2, k)
    fwd_mirror(4)
    fwd_mirror(5)
    for h in range(HALVES):
        w_wait(h, far, F_OWN)
        w_wait(h, p_far, F_P)
    for j in range(ZN):
        for k in range(YN):
            tok_wait(at_ex(z - j, y - k, 1 - c), TS(j, k))
    for cp in keeps:
        cp.wait()
    for cp in sent:
        cp.wait_send()


def gather_all(tokens, w_in, m_in, v_in, g_in, w_out, m_out, v_out, g_out):
    rows_in, wide = w_in.shape
    rows_out, width = w_out.shape
    groups, dps = lax.axis_size("expert"), lax.axis_size("dp")
    any_space = pl.BlockSpec(memory_space=pl.ANY)
    f32, bf16 = jnp.float32, jnp.bfloat16
    return pl.pallas_call(
        gather_kernel,
        out_shape=(
            jax.ShapeDtypeStruct((2, dps, rows_in // 2, wide), bf16),
            jax.ShapeDtypeStruct((dps, rows_out, width), bf16),
            jax.ShapeDtypeStruct((groups,) + tokens.shape, bf16),
        ),
        in_specs=[any_space] * 9,
        out_specs=(any_space,) * 3,
        scratch_shapes=[pltpu.VMEM((rows_in, wide), t) for t in (f32, f32, f32, bf16)]
        + [pltpu.VMEM((rows_out, width), t) for t in (f32, f32, f32, bf16)]
        + [pltpu.VMEM((rows_in, wide), bf16), pltpu.VMEM((rows_out, width), bf16)]
        + [
            pltpu.SemaphoreType.DMA((HALVES, 4)),
            pltpu.SemaphoreType.DMA((HALVES + 1,)),
            pltpu.SemaphoreType.DMA((7 * HALVES,)),
            pltpu.SemaphoreType.DMA((7 * HALVES,)),
            pltpu.SemaphoreType.DMA((31,)),
            pltpu.SemaphoreType.DMA((31,)),
        ],
        name="update_and_gather",
        compiler_params=pltpu.CompilerParams(
            collective_id=0, has_side_effects=True, vmem_limit_bytes=24 * 2**20
        ),
    )(tokens, w_in, m_in, v_in, g_in, w_out, m_out, v_out, g_out)


def per_device(tokens, routes, route_weight, w_in, m_in, v_in, g_in, w_out, m_out, v_out, g_out):
    groups = lax.axis_size("expert")
    mine = lax.axis_index("expert")
    tok_rows, width = tokens.shape
    top_count = routes.shape[1]
    capacity = 2 * tok_rows * top_count // groups
    two, depth, wide = w_in.shape[1:]
    gu, dn, tok_all = gather_all(
        tokens,
        *(a.reshape(two * depth, wide) for a in (w_in, m_in, v_in, g_in)),
        *(a.reshape(a.shape[1:]) for a in (w_out, m_out, v_out, g_out)),
    )
    gate_up = gu.reshape(two, -1, wide)
    down = dn.reshape(-1, width)
    routes_t = routes.T
    routes_all = lax.all_gather(routes_t, "expert", axis=0)
    upper = (
        jnp.arange(tok_rows)[:, None] < jnp.arange(tok_rows)[None, :]
    ).astype(jnp.bfloat16)

    def ranks(hit):
        return jnp.dot(hit.astype(jnp.bfloat16), upper, preferred_element_type=jnp.float32).astype(jnp.int32)

    hit = jnp.any(routes_all == mine, axis=1)
    rank = ranks(hit)
    slots = jnp.arange(capacity, dtype=jnp.int32)
    pick = (hit[:, None, :] & (rank[:, None, :] == slots[None, :, None])).astype(jnp.bfloat16)
    rows = lax.dot_general(
        pick, tok_all, (((2,), (1,)), ((0,), (0,))), preferred_element_type=jnp.float32
    ).astype(jnp.bfloat16)
    rows = rows.reshape(groups * capacity, width)
    gate_pre = jnp.dot(rows, gate_up[0], preferred_element_type=jnp.float32)
    up_pre = jnp.dot(rows, gate_up[1], preferred_element_type=jnp.float32)
    hidden = (jax.nn.silu(gate_pre) * up_pre).astype(jnp.bfloat16)
    results = jnp.dot(hidden, down, preferred_element_type=jnp.float32).astype(jnp.bfloat16)
    returned = lax.all_to_all(
        results.reshape(groups, capacity, width), "expert", split_axis=0, concat_axis=0, tiled=True
    )
    named = routes_t[None, :, :] == jnp.arange(groups, dtype=jnp.int32)[:, None, None]
    out_hit = jnp.any(named, axis=1)
    out_rank = ranks(out_hit)
    weight = jnp.sum(jnp.where(named, route_weight.T[None], 0.0), axis=1)
    place = out_hit[:, None, :] & (out_rank[:, None, :] == slots[None, :, None])
    spread = jnp.where(place, weight[:, None, :], 0.0).reshape(groups * capacity, tok_rows)
    high = spread.astype(jnp.bfloat16)
    low = (spread - high.astype(jnp.float32)).astype(jnp.bfloat16)
    back = returned.reshape(groups * capacity, width)
    mixed = lax.dot_general(
        high, back, (((0,), (0,)), ((), ())), preferred_element_type=jnp.float32
    ) + lax.dot_general(low, back, (((0,), (0,)), ((), ())), preferred_element_type=jnp.float32)
    return mixed.astype(jnp.bfloat16)


def solution(mesh):
    placed = (
        P(("dp", "expert"), None),
        P(("dp", "expert"), None),
        P(("dp", "expert"), None),
        P("expert", None, "dp", None),
        P("expert", None, "dp", None),
        P("expert", None, "dp", None),
        P("expert", None, "dp", None),
        P("expert", "dp", None),
        P("expert", "dp", None),
        P("expert", "dp", None),
        P("expert", "dp", None),
    )
    return jax.shard_map(
        per_device, mesh=mesh, in_specs=placed, out_specs=P(("dp", "expert"), None), check_vma=False
    )
```

```python
import functools

import jax
import jax.numpy as jnp
from jax import lax
from jax.experimental import pallas as pl
from jax.experimental.pallas import tpu as pltpu
from jax.sharding import PartitionSpec as P

MESH = pl.DeviceIdType.MESH
beta_one = 0.9
beta_two = 0.95
corr_one = 0.99997343860111
corr_two = 0.99407947077967
adam_eps = 1e-08
learn_rate = 0.01
weight_decay = 0.1
XN, YN, ZN = 4, 4, 4
HALVES = 6


def adamw(master, moment, second, gradient):
    grad_value = gradient.astype(jnp.float32)
    moment_new = beta_one * moment + (1.0 - beta_one) * grad_value
    second_new = beta_two * second + (1.0 - beta_two) * grad_value * grad_value
    update = moment_new / corr_one / (jnp.sqrt(second_new / corr_two) + adam_eps)
    return (master - learn_rate * (update + weight_decay * master)).astype(jnp.bfloat16)


def gather_kernel(
    tok, w_in, m_in, v_in, g_in, w_out, m_out, v_out, g_out,
    gu_all, dn_all, tok_all,
    wi, mi, vi, gi, wo, mo, vo, go, gu_own, dn_own,
    load_sem, keep_sem, w_send, w_recv, t_send, t_recv,
):
    d, e = lax.axis_index("dp"), lax.axis_index("expert")
    zh, x = d // XN, d % XN
    z, y, c = e // (2 * YN), e // 2 % YN, e % 2
    at_dp = lambda h, i: h * XN + lax.rem(i + XN, XN)
    right, left, far = at_dp(zh, x + 1), at_dp(zh, x - 1), at_dp(zh, x + 2)
    mirror = at_dp(1 - zh, x)
    p_right, p_left, p_far = at_dp(1 - zh, x + 1), at_dp(1 - zh, x - 1), at_dp(1 - zh, x + 2)
    at_ex = lambda zz, yy, cc: lax.rem(zz + ZN, ZN) * (2 * YN) + lax.rem(yy + YN, YN) * 2 + cc

    half_in, half_out = w_in.shape[0] // 4, w_out.shape[0] // 2
    loads = []
    for h in range(HALVES):
        pairs = (
            ((w_in, wi), (m_in, mi), (v_in, vi), (g_in, gi))
            if h < 4
            else ((w_out, wo), (m_out, mo), (v_out, vo), (g_out, go))
        )
        rows = pl.ds(h * half_in, half_in) if h < 4 else pl.ds((h - 4) * half_out, half_out)
        loads.append(
            [pltpu.make_async_copy(a.at[rows], b.at[rows], load_sem.at[h, i]) for i, (a, b) in enumerate(pairs)]
        )
        for cp in loads[h]:
            cp.start()

    barrier = pltpu.get_barrier_semaphore()
    partners = [{"dp": p, "expert": e} for p in (right, left, mirror)]
    partners += [{"dp": d, "expert": at_ex(z, y + k, c)} for k in range(1, YN)]
    partners += [{"dp": d, "expert": p} for p in (at_ex(z, y, 1 - c), at_ex(z + 1, y, c), at_ex(z - 1, y, c))]
    for p in partners:
        pl.semaphore_signal(barrier, inc=1, device_id=p, device_id_type=MESH)
    pl.semaphore_wait(barrier, len(partners))

    sent = []

    def tok_copy(slot, target, op, src=None):
        return pltpu.make_async_remote_copy(
            src_ref=tok_all.at[slot] if src is None else src, dst_ref=tok_all.at[slot],
            send_sem=t_send.at[op], recv_sem=t_recv.at[op],
            device_id={"dp": d, "expert": target}, device_id_type=MESH,
        )

    UP = lambda n: n - 1
    DOWN = lambda n: 2 + n
    TY = lambda b, k: 6 + b * 3 + k - 1
    TS = lambda b, k: 18 + b * 4 + k
    sibling = at_ex(z, y, 1 - c)

    def tok_spread(b, src=None):
        slot = at_ex(b, y, c)
        for k in (1, 3, 2):
            tok_copy(slot, at_ex(z, y + k, c), TY(b, k), src).start()
        tok_copy(slot, sibling, TS(b, 0), src).start()

    own_tok = pltpu.make_async_copy(tok, tok_all.at[e], keep_sem.at[0])
    own_tok.start()
    can_up, can_down = z < ZN - 1, z > 0

    @pl.when(can_up)
    def _():
        tok_copy(e, at_ex(z + 1, y, c), UP(1), tok).start()

    @pl.when(can_down)
    def _():
        tok_copy(e, at_ex(z - 1, y, c), DOWN(1), tok).start()

    tok_spread(z, tok)

    def tok_z(n):
        @pl.when(z >= n)
        def _():
            slot = at_ex(z - n, y, c)
            tok_copy(slot, sibling, UP(n)).wait_recv()

            if n < ZN - 1:

                @pl.when(can_up)
                def _():
                    tok_copy(slot, at_ex(z + 1, y, c), UP(n + 1)).start()

            tok_spread(z - n)

        @pl.when(z < ZN - n)
        def _():
            slot = at_ex(z + n, y, c)
            tok_copy(slot, sibling, DOWN(n)).wait_recv()

            if n < ZN - 1:

                @pl.when(can_down)
                def _():
                    tok_copy(slot, at_ex(z - 1, y, c), DOWN(n + 1)).start()

            tok_spread(z + n)

    def tok_y(n):
        def hand_on(b):
            for k in (1, 3, 2):
                slot = at_ex(b, y - k, c)
                tok_copy(slot, sibling, TY(b, k)).wait_recv()
                tok_copy(slot, sibling, TS(b, k)).start()

        if n == 0:
            hand_on(z)
            return
        pl.when(z >= n)(lambda: hand_on(z - n))
        pl.when(z < ZN - n)(lambda: hand_on(z + n))

    def tok_finish():
        for b in range(ZN):
            for k in range(YN):
                tok_copy(at_ex(b, y - k, 1 - c), sibling, TS(b, k)).wait_recv()
        for b in range(ZN):
            for k in range(1, YN):
                tok_copy(e, sibling, TY(b, k)).wait_send()
            for k in range(YN):
                tok_copy(e, sibling, TS(b, k)).wait_send()
        for n in range(1, ZN):

            @pl.when(jnp.logical_and(can_up, z >= n - 1))
            def _():
                tok_copy(e, sibling, UP(n)).wait_send()

            @pl.when(jnp.logical_and(can_down, z <= ZN - n))
            def _():
                tok_copy(e, sibling, DOWN(n)).wait_send()

    def slot_of(h, owner):
        if h < 4:
            return gu_all.at[h // 2, owner, pl.ds(h % 2 * half_in, half_in)]
        return dn_all.at[owner, pl.ds((h - 4) * half_out, half_out)]

    def own_of(h):
        return gu_own.at[pl.ds(h * half_in, half_in)] if h < 4 else dn_own.at[pl.ds((h - 4) * half_out, half_out)]

    def w_copy(h, owner, target, kind, src=None):
        op = kind * HALVES + h
        return pltpu.make_async_remote_copy(
            src_ref=slot_of(h, owner) if src is None else src, dst_ref=slot_of(h, owner),
            send_sem=w_send.at[op], recv_sem=w_recv.at[op],
            device_id={"dp": target, "expert": e}, device_id_type=MESH,
        )

    R_OWN, L_OWN, MIR, F_OWN, R_P, L_P, F_P = range(7)

    def w_send_to(h, owner, target, kind, src=None):
        cp = w_copy(h, owner, target, kind, src)
        cp.start()
        sent.append(cp)

    def w_wait(h, owner, kind):
        w_copy(h, owner, right, kind).wait_recv()

    keeps = [own_tok]
    for h in range(HALVES):
        for cp in loads[h]:
            cp.wait()
        a, b, v, g, out, rows, first = (
            (wi, mi, vi, gi, gu_own, half_in, h * half_in)
            if h < 4
            else (wo, mo, vo, go, dn_own, half_out, (h - 4) * half_out)
        )

        def step(i, _, a=a, b=b, v=v, g=g, out=out, first=first):
            at = pl.ds(pl.multiple_of(first + i * 16, 16), 16)
            out[at, :] = adamw(a[at, :], b[at, :], v[at, :], g[at, :])
            return 0

        lax.fori_loop(0, rows // 16, step, 0)
        if h < 2:
            w_copy(h, d, mirror, MIR, own_of(h)).start()
        w_send_to(h, d, right, R_OWN, own_of(h))
        w_send_to(h, d, left, L_OWN, own_of(h))
        keep = pltpu.make_async_copy(own_of(h), slot_of(h, d), keep_sem.at[1 + h])
        keep.start()
        keeps.append(keep)

    def fwd_own(h):
        w_wait(h, left, R_OWN)
        w_wait(h, right, L_OWN)
        if h % 2 == 0:
            w_send_to(h, left, right, F_OWN)
        else:
            w_send_to(h, right, left, F_OWN)

    def to_mirror(h):
        w_copy(h - 2, d, mirror, MIR, own_of(h - 2)).wait_send()
        w_copy(h, d, mirror, MIR, own_of(h)).start()

    def from_mirror(h):
        w_wait(h, mirror, MIR)
        w_send_to(h, mirror, right, R_P)
        w_send_to(h, mirror, left, L_P)

    def fwd_mirror(h):
        w_wait(h, p_left, R_P)
        w_wait(h, p_right, L_P)
        if h % 2 == 0:
            w_send_to(h, p_left, right, F_P)
        else:
            w_send_to(h, p_right, left, F_P)

    tok_z(1)
    fwd_own(0)
    fwd_own(1)
    to_mirror(2)
    tok_z(2)
    fwd_own(2)
    fwd_own(3)
    to_mirror(3)
    tok_z(3)
    fwd_own(4)
    fwd_own(5)
    from_mirror(0)
    to_mirror(4)
    tok_y(0)
    from_mirror(1)
    fwd_mirror(0)
    to_mirror(5)
    tok_y(1)
    from_mirror(2)
    fwd_mirror(1)
    tok_y(2)
    from_mirror(3)
    fwd_mirror(2)
    tok_y(3)
    from_mirror(4)
    fwd_mirror(3)
    from_mirror(5)
    fwd_mirror(4)
    fwd_mirror(5)
    for h in range(HALVES):
        w_wait(h, far, F_OWN)
        w_wait(h, p_far, F_P)
    for h in (4, 5):
        w_copy(h, d, mirror, MIR, own_of(h)).wait_send()
    tok_finish()
    for cp in keeps:
        cp.wait()
    for cp in sent:
        cp.wait_send()


def gather_all(tokens, w_in, m_in, v_in, g_in, w_out, m_out, v_out, g_out):
    rows_in, wide = w_in.shape
    rows_out, width = w_out.shape
    groups, dps = lax.axis_size("expert"), lax.axis_size("dp")
    any_space = pl.BlockSpec(memory_space=pl.ANY)
    f32, bf16 = jnp.float32, jnp.bfloat16
    return pl.pallas_call(
        gather_kernel,
        out_shape=(
            jax.ShapeDtypeStruct((2, dps, rows_in // 2, wide), bf16),
            jax.ShapeDtypeStruct((dps, rows_out, width), bf16),
            jax.ShapeDtypeStruct((groups,) + tokens.shape, bf16),
        ),
        in_specs=[any_space] * 9,
        out_specs=(any_space,) * 3,
        scratch_shapes=[pltpu.VMEM((rows_in, wide), t) for t in (f32, f32, f32, bf16)]
        + [pltpu.VMEM((rows_out, width), t) for t in (f32, f32, f32, bf16)]
        + [pltpu.VMEM((rows_in, wide), bf16), pltpu.VMEM((rows_out, width), bf16)]
        + [
            pltpu.SemaphoreType.DMA((HALVES, 4)),
            pltpu.SemaphoreType.DMA((HALVES + 1,)),
            pltpu.SemaphoreType.DMA((7 * HALVES,)),
            pltpu.SemaphoreType.DMA((7 * HALVES,)),
            pltpu.SemaphoreType.DMA((34,)),
            pltpu.SemaphoreType.DMA((34,)),
        ],
        name="update_and_gather",
        compiler_params=pltpu.CompilerParams(
            collective_id=0, has_side_effects=True, vmem_limit_bytes=60 * 2**20
        ),
    )(tokens, w_in, m_in, v_in, g_in, w_out, m_out, v_out, g_out)


def per_device(tokens, routes, route_weight, w_in, m_in, v_in, g_in, w_out, m_out, v_out, g_out):
    groups = lax.axis_size("expert")
    mine = lax.axis_index("expert")
    tok_rows, width = tokens.shape
    top_count = routes.shape[1]
    capacity = 2 * tok_rows * top_count // groups
    two, depth, wide = w_in.shape[1:]
    whole = -(-(width + 3 * top_count) // 128) * 128
    high = lax.reduce_precision(route_weight, 8, 7)
    low = route_weight - high
    packed = [tokens] + [a.astype(jnp.bfloat16) for a in (routes, high, low)]
    packed += [jnp.zeros((tok_rows, whole - width - 3 * top_count), jnp.bfloat16)]
    gu, dn, tok_all = gather_all(
        jnp.concatenate(packed, axis=1),
        *(a.reshape(two * depth, wide) for a in (w_in, m_in, v_in, g_in)),
        *(a.reshape(a.shape[1:]) for a in (w_out, m_out, v_out, g_out)),
    )
    gate_up = gu.reshape(two, -1, wide)
    down = dn.reshape(-1, width)
    routes_t = routes.T
    routes_all = tok_all[:, :, width : width + top_count].astype(jnp.int32)
    upper = (
        jnp.arange(tok_rows)[:, None] < jnp.arange(tok_rows)[None, :]
    ).astype(jnp.bfloat16)

    def ranks(hit):
        return jnp.dot(hit.astype(jnp.bfloat16), upper, preferred_element_type=jnp.float32).astype(jnp.int32)

    hit = jnp.any(routes_all == mine, axis=2)
    rank = ranks(hit)
    slots = jnp.arange(capacity, dtype=jnp.int32)
    pick = (hit[:, None, :] & (rank[:, None, :] == slots[None, :, None])).astype(jnp.bfloat16)
    rows = lax.dot_general(
        pick, tok_all[:, :, :width], (((2,), (1,)), ((0,), (0,))), preferred_element_type=jnp.float32
    ).astype(jnp.bfloat16)
    rows = rows.reshape(groups * capacity, width)
    gate_pre = jnp.dot(rows, gate_up[0], preferred_element_type=jnp.float32)
    up_pre = jnp.dot(rows, gate_up[1], preferred_element_type=jnp.float32)
    hidden = (jax.nn.silu(gate_pre) * up_pre).astype(jnp.bfloat16)
    results = jnp.dot(hidden, down, preferred_element_type=jnp.float32).astype(jnp.bfloat16)
    returned = lax.all_to_all(
        results.reshape(groups, capacity, width), "expert", split_axis=0, concat_axis=0, tiled=True
    )
    named = routes_t[None, :, :] == jnp.arange(groups, dtype=jnp.int32)[:, None, None]
    out_hit = jnp.any(named, axis=1)
    out_rank = ranks(out_hit)
    weight = jnp.sum(jnp.where(named, route_weight.T[None], 0.0), axis=1)
    place = out_hit[:, None, :] & (out_rank[:, None, :] == slots[None, :, None])
    spread = jnp.where(place, weight[:, None, :], 0.0).reshape(groups * capacity, tok_rows)
    high = spread.astype(jnp.bfloat16)
    low = (spread - high.astype(jnp.float32)).astype(jnp.bfloat16)
    back = returned.reshape(groups * capacity, width)
    mixed = lax.dot_general(
        high, back, (((0,), (0,)), ((), ())), preferred_element_type=jnp.float32
    ) + lax.dot_general(low, back, (((0,), (0,)), ((), ())), preferred_element_type=jnp.float32)
    return mixed.astype(jnp.bfloat16)


def solution(mesh):
    placed = (
        P(("dp", "expert"), None),
        P(("dp", "expert"), None),
        P(("dp", "expert"), None),
        P("expert", None, "dp", None),
        P("expert", None, "dp", None),
        P("expert", None, "dp", None),
        P("expert", None, "dp", None),
        P("expert", "dp", None),
        P("expert", "dp", None),
        P("expert", "dp", None),
        P("expert", "dp", None),
    )
    return jax.shard_map(
        per_device, mesh=mesh, in_specs=placed, out_specs=P(("dp", "expert"), None), check_vma=False
    )
```

```python
import jax
import jax.numpy as jnp
from jax import lax
from jax.experimental import pallas as pl
from jax.experimental.pallas import tpu as pltpu
from jax.sharding import PartitionSpec as P

MESH = pl.DeviceIdType.MESH
beta_one = 0.9
beta_two = 0.95
corr_one = 0.99997343860111
corr_two = 0.99407947077967
adam_eps = 1e-08
learn_rate = 0.01
weight_decay = 0.1
XN, YN, ZN = 4, 4, 4
TOPW = 4
HALVES = 6


def adamw(master, moment, second, gradient):
    grad_value = gradient.astype(jnp.float32)
    moment_new = beta_one * moment + (1.0 - beta_one) * grad_value
    second_new = beta_two * second + (1.0 - beta_two) * grad_value * grad_value
    update = moment_new / corr_one / (jnp.sqrt(second_new / corr_two) + adam_eps)
    return (master - learn_rate * (update + weight_decay * master)).astype(jnp.bfloat16)


def layer_kernel(
    tok, w_in, m_in, v_in, g_in, w_out, m_out, v_out, g_out,
    mixed, tok_all,
    wi, mi, vi, gi, wo, mo, vo, go, gu_v, dn_v,
    tbuf, meta, rows_v, gate_v, hid_v, res_v, ry_v, part_v, sib_v, sum_v, zin_v,
    load_sem, keep_sem, w_send, w_recv, t_send, t_recv, tin_sem, y_send, y_recv, s_send, s_recv, z_send, z_recv,
):
    d, e = lax.axis_index("dp"), lax.axis_index("expert")
    zh, x = d // XN, d % XN
    z, y, c = e // (2 * YN), e // 2 % YN, e % 2
    at_dp = lambda h, i: h * XN + lax.rem(i + XN, XN)
    right, left, far = at_dp(zh, x + 1), at_dp(zh, x - 1), at_dp(zh, x + 2)
    mirror = at_dp(1 - zh, x)
    p_right, p_left, p_far = at_dp(1 - zh, x + 1), at_dp(1 - zh, x - 1), at_dp(1 - zh, x + 2)
    at_ex = lambda zz, yy, cc: lax.rem(zz + ZN, ZN) * (2 * YN) + lax.rem(yy + YN, YN) * 2 + cc

    half_in, half_out = w_in.shape[0] // 4, w_out.shape[0] // 2
    loads = []
    for h in range(HALVES):
        pairs = (
            ((w_in, wi), (m_in, mi), (v_in, vi), (g_in, gi))
            if h < 4
            else ((w_out, wo), (m_out, mo), (v_out, vo), (g_out, go))
        )
        rows = pl.ds(h * half_in, half_in) if h < 4 else pl.ds((h - 4) * half_out, half_out)
        loads.append(
            [pltpu.make_async_copy(a.at[rows], b.at[rows], load_sem.at[h, i]) for i, (a, b) in enumerate(pairs)]
        )
        for cp in loads[h]:
            cp.start()

    barrier = pltpu.get_barrier_semaphore()
    partners = [{"dp": p, "expert": e} for p in (right, left, mirror)]
    partners += [{"dp": d, "expert": at_ex(z, y + k, c)} for k in range(1, YN)]
    partners += [{"dp": d, "expert": at_ex(z + k, y, c)} for k in range(1, ZN)]
    partners += [{"dp": d, "expert": at_ex(z, y, 1 - c)}]
    for p in partners:
        pl.semaphore_signal(barrier, inc=1, device_id=p, device_id_type=MESH)
    pl.semaphore_wait(barrier, len(partners))

    sent = []

    def tok_copy(slot, target, op, src=None):
        return pltpu.make_async_remote_copy(
            src_ref=tok_all.at[slot] if src is None else src, dst_ref=tok_all.at[slot],
            send_sem=t_send.at[op], recv_sem=t_recv.at[op],
            device_id={"dp": d, "expert": target}, device_id_type=MESH,
        )

    UP = lambda n: n - 1
    DOWN = lambda n: 2 + n
    TY = lambda b, k: 6 + b * 3 + k - 1
    TS = lambda b, k: 18 + b * 4 + k
    sibling = at_ex(z, y, 1 - c)

    def tok_spread(b, src=None):
        slot = at_ex(b, y, c)
        for k in (1, 3, 2):
            tok_copy(slot, at_ex(z, y + k, c), TY(b, k), src).start()
        tok_copy(slot, sibling, TS(b, 0), src).start()

    own_tok = pltpu.make_async_copy(tok, tok_all.at[e], keep_sem.at[0])
    own_tok.start()
    can_up, can_down = z < ZN - 1, z > 0

    @pl.when(can_up)
    def _():
        tok_copy(e, at_ex(z + 1, y, c), UP(1), tok).start()

    @pl.when(can_down)
    def _():
        tok_copy(e, at_ex(z - 1, y, c), DOWN(1), tok).start()

    tok_spread(z, tok)

    def tok_z(n):
        @pl.when(z >= n)
        def _():
            slot = at_ex(z - n, y, c)
            tok_copy(slot, sibling, UP(n)).wait_recv()

            if n < ZN - 1:

                @pl.when(can_up)
                def _():
                    tok_copy(slot, at_ex(z + 1, y, c), UP(n + 1)).start()

            tok_spread(z - n)

        @pl.when(z < ZN - n)
        def _():
            slot = at_ex(z + n, y, c)
            tok_copy(slot, sibling, DOWN(n)).wait_recv()

            if n < ZN - 1:

                @pl.when(can_down)
                def _():
                    tok_copy(slot, at_ex(z - 1, y, c), DOWN(n + 1)).start()

            tok_spread(z + n)

    def tok_y(n):
        def hand_on(b):
            for k in (1, 3, 2):
                slot = at_ex(b, y - k, c)
                tok_copy(slot, sibling, TY(b, k)).wait_recv()
                tok_copy(slot, sibling, TS(b, k)).start()

        if n == 0:
            hand_on(z)
            return
        pl.when(z >= n)(lambda: hand_on(z - n))
        pl.when(z < ZN - n)(lambda: hand_on(z + n))

    def tok_arrive():
        for b in range(ZN):
            for k in range(YN):
                tok_copy(at_ex(b, y - k, 1 - c), sibling, TS(b, k)).wait_recv()

    def tok_finish():
        for b in range(ZN):
            for k in range(1, YN):
                tok_copy(e, sibling, TY(b, k)).wait_send()
            for k in range(YN):
                tok_copy(e, sibling, TS(b, k)).wait_send()
        for n in range(1, ZN):

            @pl.when(jnp.logical_and(can_up, z >= n - 1))
            def _():
                tok_copy(e, sibling, UP(n)).wait_send()

            @pl.when(jnp.logical_and(can_down, z <= ZN - n))
            def _():
                tok_copy(e, sibling, DOWN(n)).wait_send()

    def slot_of(h, owner):
        if h < 4:
            first = pl.multiple_of(owner * (2 * half_in) + h % 2 * half_in, 16)
            return gu_v.at[h // 2, pl.ds(first, half_in)]
        first = pl.multiple_of(owner * (2 * half_out) + (h - 4) * half_out, 16)
        return dn_v.at[pl.ds(first, half_out)]

    def w_copy(h, owner, target, kind):
        op = kind * HALVES + h
        return pltpu.make_async_remote_copy(
            src_ref=slot_of(h, owner), dst_ref=slot_of(h, owner),
            send_sem=w_send.at[op], recv_sem=w_recv.at[op],
            device_id={"dp": target, "expert": e}, device_id_type=MESH,
        )

    R_OWN, L_OWN, MIR, F_OWN, R_P, L_P, F_P = range(7)

    def w_send_to(h, owner, target, kind):
        cp = w_copy(h, owner, target, kind)
        cp.start()
        sent.append(cp)

    def w_wait(h, owner, kind):
        w_copy(h, owner, right, kind).wait_recv()

    for h in range(HALVES):
        for cp in loads[h]:
            cp.wait()
        a, b, v, g, out, count, first = (
            (wi, mi, vi, gi, gu_v.at[h // 2], half_in, h * half_in)
            if h < 4
            else (wo, mo, vo, go, dn_v, half_out, (h - 4) * half_out)
        )
        base = d * (2 * half_in) + h % 2 * half_in if h < 4 else d * (2 * half_out) + (h - 4) * half_out

        def step(i, _, a=a, b=b, v=v, g=g, out=out, first=first, base=base):
            at = pl.ds(pl.multiple_of(first + i * 16, 16), 16)
            out[pl.ds(pl.multiple_of(base + i * 16, 16), 16), :] = adamw(a[at, :], b[at, :], v[at, :], g[at, :])
            return 0

        lax.fori_loop(0, count // 16, step, 0)
        if h < 2:
            w_copy(h, d, mirror, MIR).start()
        w_send_to(h, d, right, R_OWN)
        w_send_to(h, d, left, L_OWN)

    def fwd_own(h):
        w_wait(h, left, R_OWN)
        w_wait(h, right, L_OWN)
        if h % 2 == 0:
            w_send_to(h, left, right, F_OWN)
        else:
            w_send_to(h, right, left, F_OWN)

    def to_mirror(h):
        w_copy(h - 2, d, mirror, MIR).wait_send()
        w_copy(h, d, mirror, MIR).start()

    def from_mirror(h):
        w_wait(h, mirror, MIR)
        w_send_to(h, mirror, right, R_P)
        w_send_to(h, mirror, left, L_P)

    def fwd_mirror(h):
        w_wait(h, p_left, R_P)
        w_wait(h, p_right, L_P)
        if h % 2 == 0:
            w_send_to(h, p_left, right, F_P)
        else:
            w_send_to(h, p_right, left, F_P)

    width, wide = dn_v.shape[1], dn_v.shape[0]
    tok_rows = tok.shape[0]
    blocks = tok_all.shape[0]
    cap = rows_v.shape[0] // blocks
    f32, bf16 = jnp.float32, jnp.bfloat16

    def iota(shape, dim):
        return lax.broadcasted_iota(jnp.int32, shape, dim)

    def routed(info, expert, slot):
        lanes = expert.shape[1]
        hit = jnp.zeros((tok_rows, lanes), f32)
        weight = jnp.zeros((tok_rows, lanes), f32)
        for k in range(TOPW):
            same = info[:, k : k + 1] == expert
            hit = jnp.where(same, 1.0, hit)
            share = info[:, TOPW + k : TOPW + k + 1] + info[:, 2 * TOPW + k : 2 * TOPW + k + 1]
            weight = jnp.where(same, share, weight)
        earlier = (iota((tok_rows, tok_rows), 1) < iota((tok_rows, tok_rows), 0)).astype(bf16)
        rank = jnp.dot(earlier, hit.astype(bf16), preferred_element_type=f32)
        return jnp.logical_and(rank == slot, hit > 0.0), weight

    def tok_in(s):
        return pltpu.make_async_copy(tok_all.at[s], tbuf.at[lax.rem(s, 2)], tin_sem.at[lax.rem(s, 2)])

    def pick_rows():
        tok_in(0).start()

        def step(s, _):
            @pl.when(s < blocks - 1)
            def _():
                tok_in(s + 1).start()

            tok_in(s).wait()
            at = lax.rem(s, 2)
            info = tbuf[at, :, width:]
            meta[s] = info
            ours = jnp.zeros((1, cap), f32) + e.astype(f32)
            place, _ = routed(info.astype(f32), ours, iota((1, cap), 1).astype(f32))
            picked = lax.dot_general(
                jnp.where(place, 1.0, 0.0).astype(bf16), tbuf[at, :, :width],
                (((0,), (0,)), ((), ())), preferred_element_type=f32,
            )
            rows_v[pl.ds(pl.multiple_of(s * cap, cap), cap), :] = picked.astype(bf16)
            return 0

        lax.fori_loop(0, blocks, step, 0)

    tall, tile = 512, 256

    def up_tiles(gated):
        def step(i, _):
            at = pl.ds(pl.multiple_of(lax.rem(i, 2) * tall, tall), tall)
            cols = pl.ds(pl.multiple_of(i // 2 * tile, tile), tile)
            product = jnp.dot(rows_v[at, :], gu_v[1 if gated else 0, :, cols], preferred_element_type=f32)
            if gated:
                hid_v[at, cols] = (jax.nn.silu(gate_v[at, cols]) * product).astype(bf16)
            else:
                gate_v[at, cols] = product
            return 0

        lax.fori_loop(0, 2 * wide // tile, step, 0)

    group = rows_v.shape[0] // ZN
    pair = 2 * cap

    def y_copy(i, zt, k, to):
        return pltpu.make_async_remote_copy(
            src_ref=res_v.at[zt, pl.ds(pl.multiple_of(to * pair, pair), pair)], dst_ref=ry_v.at[zt, pl.ds(pl.multiple_of(y * pair, pair), pair)],
            send_sem=y_send.at[i, k - 1], recv_sem=y_recv.at[i, k - 1],
            device_id={"dp": d, "expert": at_ex(z, to, c)}, device_id_type=MESH,
        )

    def down(i, zt):
        def step(n, _):
            cols = pl.ds(pl.multiple_of(n * tile, tile), tile)
            mine = pl.ds(pl.multiple_of(zt * group, group), group)
            res_v[zt, :, cols] = jnp.dot(hid_v[mine, :], dn_v[:, cols], preferred_element_type=f32).astype(bf16)
            return 0

        lax.fori_loop(0, width // tile, step, 0)
        for k in (1, 3, 2):
            y_copy(i, zt, k, lax.rem(y + k, YN)).start()
        own = pl.ds(pl.multiple_of(y * pair, pair), pair)
        ry_v[zt, own, :] = res_v[zt, own, :]

    def s_copy(i, zt):
        return pltpu.make_async_remote_copy(
            src_ref=part_v.at[zt, 1 - c], dst_ref=sib_v.at[zt], send_sem=s_send.at[i], recv_sem=s_recv.at[i],
            device_id={"dp": d, "expert": sibling}, device_id_type=MESH,
        )

    def z_copy(j, zt):
        return pltpu.make_async_remote_copy(
            src_ref=sum_v.at[zt], dst_ref=zin_v.at[j - 1], send_sem=z_send.at[j - 1], recv_sem=z_recv.at[j - 1],
            device_id={"dp": d, "expert": at_ex(zt, y, c)}, device_id_type=MESH,
        )

    def partial(i, zt):
        for k in range(1, YN):
            y_copy(i, zt, k, y).wait_recv()
        lane = iota((1, YN * pair), 1)
        expert = (z * (2 * YN) + lane // pair * 2 + c).astype(f32)
        slot = lax.rem(lane, cap).astype(f32)
        spread = []
        for cc in range(2):
            place, weight = routed(meta[zt * (2 * YN) + y * 2 + cc].astype(f32), expert, slot)
            place = jnp.logical_and(place, lax.rem(lane // cap, 2) == cc)
            spread.append(jnp.where(place, weight, 0.0))
        spread = jnp.concatenate(spread, axis=0)
        high = spread.astype(bf16)
        low = (spread - high.astype(f32)).astype(bf16)

        def step(n, _):
            cols = pl.ds(pl.multiple_of(n * tile, tile), tile)
            arrived = ry_v[zt, :, cols]
            total = jnp.dot(high, arrived, preferred_element_type=f32) + jnp.dot(low, arrived, preferred_element_type=f32)
            part_v[zt, 0, :, cols] = total[:tok_rows].astype(bf16)
            part_v[zt, 1, :, cols] = total[tok_rows:].astype(bf16)
            return 0

        lax.fori_loop(0, width // tile, step, 0)
        s_copy(i, zt).start()

    def both_cores(i, zt):
        s_copy(i, zt).wait_recv()

        def step(n, _):
            at = pl.ds(pl.multiple_of(n * 16, 16), 16)
            sum_v[zt, at, :] = (part_v[zt, c, at, :].astype(f32) + sib_v[zt, at, :].astype(f32)).astype(bf16)
            return 0

        lax.fori_loop(0, tok_rows // 16, step, 0)

    tok_z(1)
    fwd_own(0)
    fwd_own(1)
    to_mirror(2)
    tok_z(2)
    fwd_own(2)
    fwd_own(3)
    to_mirror(3)
    tok_z(3)
    fwd_own(4)
    fwd_own(5)
    from_mirror(0)
    to_mirror(4)
    tok_y(0)
    from_mirror(1)
    fwd_mirror(0)
    to_mirror(5)
    tok_y(1)
    from_mirror(2)
    fwd_mirror(1)
    tok_y(2)
    tok_y(3)
    from_mirror(3)
    fwd_mirror(2)
    own_tok.wait()
    tok_arrive()
    pick_rows()
    from_mirror(4)
    fwd_mirror(3)
    for h in (0, 1):
        w_wait(h, far, F_OWN)
        w_wait(h, p_far, F_P)
    up_tiles(False)
    from_mirror(5)
    fwd_mirror(4)
    fwd_mirror(5)
    for h in (2, 3):
        w_wait(h, far, F_OWN)
        w_wait(h, p_far, F_P)
    up_tiles(True)
    for h in (4, 5):
        w_wait(h, far, F_OWN)
        w_wait(h, p_far, F_P)
    order = [(i, j, lax.rem(z + j, ZN)) for i, j in enumerate((2, 1, 3, 0))]
    for i, j, zt in order:
        down(i, zt)
    for i, j, zt in order:
        partial(i, zt)
        both_cores(i, zt)
        if j:
            z_copy(j, zt).start()
    for j in range(1, ZN):
        z_copy(j, z).wait_recv()

    def step(n, _):
        at = pl.ds(pl.multiple_of(n * 16, 16), 16)
        total = sum_v[z, at, :].astype(f32)
        for j in range(ZN - 1):
            total = total + zin_v[j, at, :].astype(f32)
        mixed[at, :] = total.astype(bf16)
        return 0

    lax.fori_loop(0, tok_rows // 16, step, 0)
    for i, j, zt in order:
        for k in range(1, YN):
            y_copy(i, zt, k, lax.rem(y + k, YN)).wait_send()
        s_copy(i, zt).wait_send()
        if j:
            z_copy(j, zt).wait_send()
    for h in (4, 5):
        w_copy(h, d, mirror, MIR).wait_send()
    tok_finish()
    for cp in sent:
        cp.wait_send()


def layer(tokens, w_in, m_in, v_in, g_in, w_out, m_out, v_out, g_out):
    rows_in, wide = w_in.shape
    rows_out, width = w_out.shape
    groups, dps = lax.axis_size("expert"), lax.axis_size("dp")
    tok_rows, whole = tokens.shape
    cap = 2 * tok_rows * TOPW // groups
    any_space = pl.BlockSpec(memory_space=pl.ANY)
    f32, bf16 = jnp.float32, jnp.bfloat16
    dma = pltpu.SemaphoreType.DMA
    mixed, _ = pl.pallas_call(
        layer_kernel,
        out_shape=(
            jax.ShapeDtypeStruct((tok_rows, width), bf16),
            jax.ShapeDtypeStruct((groups, tok_rows, whole), bf16),
        ),
        in_specs=[any_space] * 9,
        out_specs=(pl.BlockSpec(memory_space=pltpu.VMEM), any_space),
        scratch_shapes=[pltpu.VMEM((rows_in, wide), t) for t in (f32, f32, f32, bf16)]
        + [pltpu.VMEM((rows_out, width), t) for t in (f32, f32, f32, bf16)]
        + [
            pltpu.VMEM((2, dps * rows_in // 2, wide), bf16),
            pltpu.VMEM((dps * rows_out, width), bf16),
            pltpu.VMEM((2, tok_rows, whole), bf16),
            pltpu.VMEM((groups, tok_rows, whole - width), bf16),
            pltpu.VMEM((groups * cap, width), bf16),
            pltpu.VMEM((groups * cap, wide), f32),
            pltpu.VMEM((groups * cap, wide), bf16),
            pltpu.VMEM((ZN, groups * cap // ZN, width), bf16),
            pltpu.VMEM((ZN, 2 * YN * cap, width), bf16),
            pltpu.VMEM((ZN, 2, tok_rows, width), bf16),
            pltpu.VMEM((ZN, tok_rows, width), bf16),
            pltpu.VMEM((ZN, tok_rows, width), bf16),
            pltpu.VMEM((ZN - 1, tok_rows, width), bf16),
            dma((HALVES, 4)),
            dma((1,)),
            dma((7 * HALVES,)),
            dma((7 * HALVES,)),
            dma((34,)),
            dma((34,)),
            dma((2,)),
            dma((ZN, YN - 1)),
            dma((ZN, YN - 1)),
            dma((ZN,)),
            dma((ZN,)),
            dma((ZN - 1,)),
            dma((ZN - 1,)),
        ],
        name="moe_layer",
        compiler_params=pltpu.CompilerParams(
            collective_id=0, has_side_effects=True, vmem_limit_bytes=60 * 2**20
        ),
    )(tokens, w_in, m_in, v_in, g_in, w_out, m_out, v_out, g_out)
    return mixed


def per_device(tokens, routes, route_weight, w_in, m_in, v_in, g_in, w_out, m_out, v_out, g_out):
    tok_rows, width = tokens.shape
    two, depth, wide = w_in.shape[1:]
    whole = -(-(width + 3 * TOPW) // 128) * 128
    high = lax.reduce_precision(route_weight, 8, 7)
    low = route_weight - high
    packed = [tokens] + [a.astype(jnp.bfloat16) for a in (routes, high, low)]
    packed += [jnp.zeros((tok_rows, whole - width - 3 * TOPW), jnp.bfloat16)]
    return layer(
        jnp.concatenate(packed, axis=1),
        *(a.reshape(two * depth, wide) for a in (w_in, m_in, v_in, g_in)),
        *(a.reshape(a.shape[1:]) for a in (w_out, m_out, v_out, g_out)),
    )


def solution(mesh):
    placed = (
        P(("dp", "expert"), None),
        P(("dp", "expert"), None),
        P(("dp", "expert"), None),
        P("expert", None, "dp", None),
        P("expert", None, "dp", None),
        P("expert", None, "dp", None),
        P("expert", None, "dp", None),
        P("expert", "dp", None),
        P("expert", "dp", None),
        P("expert", "dp", None),
        P("expert", "dp", None),
    )
    return jax.shard_map(
        per_device, mesh=mesh, in_specs=placed, out_specs=P(("dp", "expert"), None), check_vma=False
    )
```

```python
import jax
import jax.numpy as jnp
from jax import lax
from jax.experimental import pallas as pl
from jax.experimental.pallas import tpu as pltpu
from jax.sharding import PartitionSpec as P

MESH = pl.DeviceIdType.MESH
beta_one = 0.9
beta_two = 0.95
corr_one = 0.99997343860111
corr_two = 0.99407947077967
adam_eps = 1e-08
learn_rate = 0.01
weight_decay = 0.1
XN, YN, ZN = 4, 4, 4
TOPW = 4
CHUNKS = 8


def adamw(master, moment, second, gradient):
    grad_value = gradient.astype(jnp.float32)
    moment_new = beta_one * moment + (1.0 - beta_one) * grad_value
    second_new = beta_two * second + (1.0 - beta_two) * grad_value * grad_value
    update = moment_new / corr_one / (jnp.sqrt(second_new / corr_two) + adam_eps)
    return (master - learn_rate * (update + weight_decay * master)).astype(jnp.bfloat16)


def layer_kernel(
    tokens, info_in, w_in, m_in, v_in, g_in, w_out, m_out, v_out, g_out,
    mixed, tok_all,
    wi, mi, vi, gi, wo, mo, vo, go, gu_v, dn_v,
    tok, tbuf, meta, rows_v, gate_v, hid_v, res_v, ry_v, part_v, sib_v, sum_v, zin_v,
    load_sem, keep_sem, w_send, w_recv, t_send, t_recv, tin_sem, y_send, y_recv, s_send, s_recv, z_send, z_recv,
):
    d, e = lax.axis_index("dp"), lax.axis_index("expert")
    zh, x = d // XN, d % XN
    z, y, c = e // (2 * YN), e // 2 % YN, e % 2
    at_dp = lambda h, i: h * XN + lax.rem(i + XN, XN)
    right, left, far = at_dp(zh, x + 1), at_dp(zh, x - 1), at_dp(zh, x + 2)
    mirror = at_dp(1 - zh, x)
    p_right, p_left, p_far = at_dp(1 - zh, x + 1), at_dp(1 - zh, x - 1), at_dp(1 - zh, x + 2)
    at_ex = lambda zz, yy, cc: lax.rem(zz + ZN, ZN) * (2 * YN) + lax.rem(yy + YN, YN) * 2 + cc

    share_in, share_out = w_in.shape[0] // 2, w_out.shape[0]
    half, third, rest = share_in // 2, share_out // 80 * 24, share_out // 80 * 16
    pieces = [(0, 0, half), (0, half, half), (1, 0, half), (1, half, half)]
    pieces += [(2, 0, third), (2, third, third), (2, 2 * third, rest), (2, 2 * third + rest, rest)]
    tok_rows, width = tokens.shape
    load_tok = pltpu.make_async_copy(tokens, tok.at[:, pl.ds(0, width)], keep_sem.at[1])
    load_tok.start()
    loads = []
    for h, (kind, first, count) in enumerate(pieces):
        pairs = (
            ((w_in, wi), (m_in, mi), (v_in, vi), (g_in, gi))
            if kind < 2
            else ((w_out, wo), (m_out, mo), (v_out, vo), (g_out, go))
        )
        rows = pl.ds(kind * share_in + first if kind < 2 else first, count)
        loads.append(
            [pltpu.make_async_copy(a.at[rows], b.at[rows], load_sem.at[h, i]) for i, (a, b) in enumerate(pairs)]
        )
        for cp in loads[h]:
            cp.start()
    info = info_in[...]
    info_high = info.astype(jnp.bfloat16).astype(jnp.float32)
    info = jnp.concatenate(
        [info_high, info - info_high, jnp.zeros((tok_rows - 2 * info.shape[0], tok_rows), jnp.float32)], axis=0
    )
    tok[:, width:] = info.T.astype(jnp.bfloat16)

    @pl.when(z == 0)
    def _():
        zin_v[:ZN] = jnp.zeros((ZN,) + zin_v.shape[1:], zin_v.dtype)

    @pl.when(z == ZN - 1)
    def _():
        zin_v[ZN:] = jnp.zeros((ZN,) + zin_v.shape[1:], zin_v.dtype)

    barrier = pltpu.get_barrier_semaphore()
    partners = [{"dp": p, "expert": e} for p in (right, left, mirror)]
    partners += [{"dp": d, "expert": at_ex(z, y + k, c)} for k in range(1, YN)]
    partners += [{"dp": d, "expert": at_ex(z + k, y, c)} for k in range(1, ZN)]
    partners += [{"dp": d, "expert": at_ex(z, y, 1 - c)}]
    for p in partners:
        pl.semaphore_signal(barrier, inc=1, device_id=p, device_id_type=MESH)
    pl.semaphore_wait(barrier, len(partners))

    sent = []

    def tok_copy(slot, target, op, src=None):
        return pltpu.make_async_remote_copy(
            src_ref=tok_all.at[slot] if src is None else src, dst_ref=tok_all.at[slot],
            send_sem=t_send.at[op], recv_sem=t_recv.at[op],
            device_id={"dp": d, "expert": target}, device_id_type=MESH,
        )

    UP = lambda n: n - 1
    DOWN = lambda n: 2 + n
    TY = lambda b, k: 6 + b * 3 + k - 1
    TS = lambda b, k: 18 + b * 4 + k
    sibling = at_ex(z, y, 1 - c)

    def tok_spread(b, src=None):
        slot = at_ex(b, y, c)
        for k in (1, 3, 2):
            tok_copy(slot, at_ex(z, y + k, c), TY(b, k), src).start()
        tok_copy(slot, sibling, TS(b, 0), src).start()

    load_tok.wait()
    own_tok = pltpu.make_async_copy(tok, tok_all.at[e], keep_sem.at[0])
    own_tok.start()
    can_up, can_down = z < ZN - 1, z > 0

    @pl.when(can_up)
    def _():
        tok_copy(e, at_ex(z + 1, y, c), UP(1), tok).start()

    @pl.when(can_down)
    def _():
        tok_copy(e, at_ex(z - 1, y, c), DOWN(1), tok).start()

    tok_spread(z, tok)

    def tok_z(n):
        @pl.when(z >= n)
        def _():
            slot = at_ex(z - n, y, c)
            tok_copy(slot, sibling, UP(n)).wait_recv()

            if n < ZN - 1:

                @pl.when(can_up)
                def _():
                    tok_copy(slot, at_ex(z + 1, y, c), UP(n + 1)).start()

            tok_spread(z - n)

        @pl.when(z < ZN - n)
        def _():
            slot = at_ex(z + n, y, c)
            tok_copy(slot, sibling, DOWN(n)).wait_recv()

            if n < ZN - 1:

                @pl.when(can_down)
                def _():
                    tok_copy(slot, at_ex(z - 1, y, c), DOWN(n + 1)).start()

            tok_spread(z + n)

    def tok_y(n):
        def hand_on(b):
            for k in (1, 3, 2):
                slot = at_ex(b, y - k, c)
                tok_copy(slot, sibling, TY(b, k)).wait_recv()
                tok_copy(slot, sibling, TS(b, k)).start()

        if n == 0:
            hand_on(z)
            return
        pl.when(z >= n)(lambda: hand_on(z - n))
        pl.when(z < ZN - n)(lambda: hand_on(z + n))

    def tok_finish():
        for b in range(ZN):
            for k in range(1, YN):
                tok_copy(e, sibling, TY(b, k)).wait_send()
            for k in range(YN):
                tok_copy(e, sibling, TS(b, k)).wait_send()
        for n in range(1, ZN):

            @pl.when(jnp.logical_and(can_up, z >= n - 1))
            def _():
                tok_copy(e, sibling, UP(n)).wait_send()

            @pl.when(jnp.logical_and(can_down, z <= ZN - n))
            def _():
                tok_copy(e, sibling, DOWN(n)).wait_send()

    def slot_of(h, owner):
        kind, first, count = pieces[h]
        if kind < 2:
            return gu_v.at[kind, pl.ds(pl.multiple_of(owner * share_in + first, 16), count)]
        return dn_v.at[pl.ds(pl.multiple_of(owner * share_out + first, 16), count)]

    def w_copy(h, owner, target, kind):
        op = kind * CHUNKS + h
        return pltpu.make_async_remote_copy(
            src_ref=slot_of(h, owner), dst_ref=slot_of(h, owner),
            send_sem=w_send.at[op], recv_sem=w_recv.at[op],
            device_id={"dp": target, "expert": e}, device_id_type=MESH,
        )

    R_OWN, L_OWN, MIR, F_OWN, R_P, L_P, F_P = range(7)

    def w_send_to(h, owner, target, kind):
        cp = w_copy(h, owner, target, kind)
        cp.start()
        sent.append(cp)

    def w_wait(h, owner, kind):
        w_copy(h, owner, right, kind).wait_recv()

    for h in range(CHUNKS):
        for cp in loads[h]:
            cp.wait()
        kind, start, count = pieces[h]
        a, b, v, g, out = (wi, mi, vi, gi, gu_v.at[kind]) if kind < 2 else (wo, mo, vo, go, dn_v)
        first = kind * share_in + start if kind < 2 else start
        base = d * (share_in if kind < 2 else share_out) + start

        def step(i, _, a=a, b=b, v=v, g=g, out=out, first=first, base=base):
            at = pl.ds(pl.multiple_of(first + i * 16, 16), 16)
            out[pl.ds(pl.multiple_of(base + i * 16, 16), 16), :] = adamw(a[at, :], b[at, :], v[at, :], g[at, :])
            return 0

        lax.fori_loop(0, count // 16, step, 0)
        if h < 2:
            w_copy(h, d, mirror, MIR).start()
        w_send_to(h, d, right, R_OWN)
        w_send_to(h, d, left, L_OWN)

    def fwd_own(h):
        w_wait(h, left, R_OWN)
        w_wait(h, right, L_OWN)
        if h % 2 == 0:
            w_send_to(h, left, right, F_OWN)
        else:
            w_send_to(h, right, left, F_OWN)

    def to_mirror(h):
        w_copy(h - 2, d, mirror, MIR).wait_send()
        w_copy(h, d, mirror, MIR).start()

    def from_mirror(h):
        w_wait(h, mirror, MIR)
        w_send_to(h, mirror, right, R_P)
        w_send_to(h, mirror, left, L_P)

    def fwd_mirror(h):
        w_wait(h, p_left, R_P)
        w_wait(h, p_right, L_P)
        if h % 2 == 0:
            w_send_to(h, p_left, right, F_P)
        else:
            w_send_to(h, p_right, left, F_P)

    wide = dn_v.shape[0]
    blocks = tok_all.shape[0]
    cap = rows_v.shape[0] // blocks
    f32, bf16 = jnp.float32, jnp.bfloat16

    def iota(shape, dim):
        return lax.broadcasted_iota(jnp.int32, shape, dim)

    def routed(info, expert, slot):
        lanes = expert.shape[1]
        hit = jnp.zeros((tok_rows, lanes), f32)
        weight = jnp.zeros((tok_rows, lanes), f32)
        for k in range(TOPW):
            same = info[:, k : k + 1] == expert
            hit = jnp.where(same, 1.0, hit)
            share = info[:, TOPW + k : TOPW + k + 1] + info[:, 3 * TOPW + k : 3 * TOPW + k + 1]
            weight = jnp.where(same, share, weight)
        earlier = (iota((tok_rows, tok_rows), 1) < iota((tok_rows, tok_rows), 0)).astype(bf16)
        rank = jnp.dot(earlier, hit.astype(bf16), preferred_element_type=f32)
        return jnp.logical_and(rank == slot, hit > 0.0), weight

    DEEP = 4

    def tok_in(s):
        return pltpu.make_async_copy(tok_all.at[s], tbuf.at[lax.rem(s, DEEP)], tin_sem.at[lax.rem(s, DEEP)])

    def pick_rows(b):
        per = 2 * YN
        for k in range(YN):
            tok_copy(at_ex(b, y - k, 1 - c), sibling, TS(b, k)).wait_recv()
        for i in range(DEEP - 1):
            tok_in(b * per + i).start()

        def step(i, _):
            s = b * per + i

            @pl.when(i < per - DEEP + 1)
            def _():
                tok_in(s + DEEP - 1).start()

            tok_in(s).wait()
            at = lax.rem(s, DEEP)
            info = tbuf[at, :, width:]
            meta[s] = info
            ours = jnp.zeros((1, cap), f32) + e.astype(f32)
            place, _ = routed(info.astype(f32), ours, iota((1, cap), 1).astype(f32))
            picked = lax.dot_general(
                jnp.where(place, 1.0, 0.0).astype(bf16), tbuf[at, :, :width],
                (((0,), (0,)), ((), ())), preferred_element_type=f32,
            )
            rows_v[pl.ds(pl.multiple_of(s * cap, cap), cap), :] = picked.astype(bf16)
            return 0

        lax.fori_loop(0, per, step, 0)

    tall, tile = 512, 256

    def up_tiles(gated):
        def step(i, _):
            at = pl.ds(pl.multiple_of(lax.rem(i, 2) * tall, tall), tall)
            cols = pl.ds(pl.multiple_of(i // 2 * tile, tile), tile)
            product = jnp.dot(rows_v[at, :], gu_v[1 if gated else 0, :, cols], preferred_element_type=f32)
            if gated:
                hid_v[at, cols] = (jax.nn.silu(gate_v[at, cols]) * product).astype(bf16)
            else:
                gate_v[at, cols] = product
            return 0

        lax.fori_loop(0, 2 * wide // tile, step, 0)

    group = rows_v.shape[0] // ZN
    pair = 2 * cap

    def y_copy(i, zt, k, to):
        return pltpu.make_async_remote_copy(
            src_ref=res_v.at[zt, pl.ds(pl.multiple_of(to * pair, pair), pair)], dst_ref=ry_v.at[zt, pl.ds(pl.multiple_of(y * pair, pair), pair)],
            send_sem=y_send.at[i, k - 1], recv_sem=y_recv.at[i, k - 1],
            device_id={"dp": d, "expert": at_ex(z, to, c)}, device_id_type=MESH,
        )

    def down(i, zt):
        def step(n, _):
            cols = pl.ds(pl.multiple_of(n * tile, tile), tile)
            mine = pl.ds(pl.multiple_of(zt * group, group), group)
            res_v[zt, :, cols] = jnp.dot(hid_v[mine, :], dn_v[:, cols], preferred_element_type=f32).astype(bf16)
            return 0

        lax.fori_loop(0, width // tile, step, 0)
        for k in (1, 3, 2):
            y_copy(i, zt, k, lax.rem(y + k, YN)).start()
        own = pl.ds(pl.multiple_of(y * pair, pair), pair)
        ry_v[zt, own, :] = res_v[zt, own, :]

    def s_copy(i, zt):
        return pltpu.make_async_remote_copy(
            src_ref=part_v.at[zt, 1 - c], dst_ref=sib_v.at[zt], send_sem=s_send.at[i], recv_sem=s_recv.at[i],
            device_id={"dp": d, "expert": sibling}, device_id_type=MESH,
        )

    def z_copy(zt, up):
        slot = jnp.where(up, zt, ZN + zt)
        return pltpu.make_async_remote_copy(
            src_ref=sum_v.at[zt], dst_ref=zin_v.at[slot], send_sem=z_send.at[slot], recv_sem=z_recv.at[slot],
            device_id={"dp": d, "expert": at_ex(jnp.where(up, z + 1, z - 1), y, c)}, device_id_type=MESH,
        )

    def partial(i, zt):
        for k in range(1, YN):
            y_copy(i, zt, k, y).wait_recv()
        lane = iota((1, YN * pair), 1)
        expert = (z * (2 * YN) + lane // pair * 2 + c).astype(f32)
        slot = lax.rem(lane, cap).astype(f32)
        spread = []
        for cc in range(2):
            place, weight = routed(meta[zt * (2 * YN) + y * 2 + cc].astype(f32), expert, slot)
            place = jnp.logical_and(place, lax.rem(lane // cap, 2) == cc)
            spread.append(jnp.where(place, weight, 0.0))
        spread = jnp.concatenate(spread, axis=0)
        high = spread.astype(bf16)
        low = (spread - high.astype(f32)).astype(bf16)

        def step(n, _):
            cols = pl.ds(pl.multiple_of(n * tile, tile), tile)
            arrived = ry_v[zt, :, cols]
            total = jnp.dot(high, arrived, preferred_element_type=f32) + jnp.dot(low, arrived, preferred_element_type=f32)
            part_v[zt, 0, :, cols] = total[:tok_rows].astype(bf16)
            part_v[zt, 1, :, cols] = total[tok_rows:].astype(bf16)
            return 0

        lax.fori_loop(0, width // tile, step, 0)
        s_copy(i, zt).start()

    def both_cores(i, zt, on):
        s_copy(i, zt).wait_recv()
        up = zt > z
        slot = jnp.where(up, zt, ZN + zt)
        if on:

            @pl.when(jnp.where(up, z, ZN - 1 - z) > 0)
            def _():
                z_copy(zt, up).wait_recv()

        def step(n, _):
            at = pl.ds(pl.multiple_of(n * 16, 16), 16)
            total = part_v[zt, c, at, :].astype(f32) + sib_v[zt, at, :].astype(f32)
            if on:
                sum_v[zt, at, :] = (total + zin_v[slot, at, :].astype(f32)).astype(bf16)
            else:
                mixed[at, :] = (total + zin_v[z, at, :].astype(f32) + zin_v[ZN + z, at, :].astype(f32)).astype(bf16)
            return 0

        if not on:
            pl.when(z > 0)(lambda: z_copy(z, True).wait_recv())
            pl.when(z < ZN - 1)(lambda: z_copy(z, False).wait_recv())
        lax.fori_loop(0, tok_rows // 16, step, 0)
        if on:
            z_copy(zt, up).start()

    def gate_up_arrive(*some):
        for h in some:
            w_wait(h, far, F_OWN)
            w_wait(h, p_far, F_P)

    tok_z(1)
    fwd_own(0)
    fwd_own(1)
    tok_z(2)
    fwd_own(2)
    fwd_own(3)
    from_mirror(0)
    to_mirror(2)
    tok_z(3)
    for h in range(4, CHUNKS):
        fwd_own(h)
    from_mirror(1)
    to_mirror(3)
    fwd_mirror(0)
    tok_y(0)
    tok_y(1)
    from_mirror(2)
    to_mirror(4)
    fwd_mirror(1)
    tok_y(2)
    tok_y(3)
    own_tok.wait()
    pick_rows(0)
    from_mirror(3)
    to_mirror(5)
    fwd_mirror(2)
    pick_rows(1)
    from_mirror(4)
    to_mirror(6)
    pick_rows(2)
    fwd_mirror(3)
    from_mirror(5)
    to_mirror(7)
    pick_rows(3)
    fwd_mirror(4)
    from_mirror(6)
    fwd_mirror(5)
    from_mirror(7)
    gate_up_arrive(0, 1)
    up_tiles(False)
    fwd_mirror(6)
    fwd_mirror(7)
    gate_up_arrive(2, 3)
    up_tiles(True)
    gate_up_arrive(4, 5, 6, 7)

    def by_z(*table):
        out = jnp.int32(table[-1])
        for at in range(ZN - 1):
            out = jnp.where(z == at, table[at], out)
        return out

    order = list(enumerate((by_z(3, 3, 0, 0), by_z(2, 0, 3, 1), by_z(1, 2, 1, 2), z)))
    for i, zt in order:
        down(i, zt)
    for i, zt in order:
        partial(i, zt)
        both_cores(i, zt, i < ZN - 1)
    for i, zt in order:
        for k in range(1, YN):
            y_copy(i, zt, k, lax.rem(y + k, YN)).wait_send()
        s_copy(i, zt).wait_send()
        if i < ZN - 1:
            z_copy(zt, zt > z).wait_send()
    for h in (CHUNKS - 2, CHUNKS - 1):
        w_copy(h, d, mirror, MIR).wait_send()
    tok_finish()
    for cp in sent:
        cp.wait_send()


def layer(tokens, info, w_in, m_in, v_in, g_in, w_out, m_out, v_out, g_out):
    rows_in, wide = w_in.shape
    rows_out, width = w_out.shape
    groups, dps = lax.axis_size("expert"), lax.axis_size("dp")
    tok_rows = tokens.shape[0]
    whole = width + 128
    cap = 2 * tok_rows * TOPW // groups
    any_space = pl.BlockSpec(memory_space=pl.ANY)
    f32, bf16 = jnp.float32, jnp.bfloat16
    dma = pltpu.SemaphoreType.DMA
    mixed, _ = pl.pallas_call(
        layer_kernel,
        out_shape=(
            jax.ShapeDtypeStruct((tok_rows, width), bf16),
            jax.ShapeDtypeStruct((groups, tok_rows, whole), bf16),
        ),
        in_specs=[any_space, pl.BlockSpec(memory_space=pltpu.VMEM)] + [any_space] * 8,
        out_specs=(pl.BlockSpec(memory_space=pltpu.VMEM), any_space),
        scratch_shapes=[pltpu.VMEM((rows_in, wide), t) for t in (f32, f32, f32, bf16)]
        + [pltpu.VMEM((rows_out, width), t) for t in (f32, f32, f32, bf16)]
        + [
            pltpu.VMEM((2, dps * rows_in // 2, wide), bf16),
            pltpu.VMEM((dps * rows_out, width), bf16),
            pltpu.VMEM((tok_rows, whole), bf16),
            pltpu.VMEM((4, tok_rows, whole), bf16),
            pltpu.VMEM((groups, tok_rows, whole - width), bf16),
            pltpu.VMEM((groups * cap, width), bf16),
            pltpu.VMEM((groups * cap, wide), f32),
            pltpu.VMEM((groups * cap, wide), bf16),
            pltpu.VMEM((ZN, groups * cap // ZN, width), bf16),
            pltpu.VMEM((ZN, 2 * YN * cap, width), bf16),
            pltpu.VMEM((ZN, 2, tok_rows, width), bf16),
            pltpu.VMEM((ZN, tok_rows, width), bf16),
            pltpu.VMEM((ZN, tok_rows, width), bf16),
            pltpu.VMEM((2 * ZN, tok_rows, width), bf16),
            dma((CHUNKS, 4)),
            dma((2,)),
            dma((7 * CHUNKS,)),
            dma((7 * CHUNKS,)),
            dma((34,)),
            dma((34,)),
            dma((4,)),
            dma((ZN, YN - 1)),
            dma((ZN, YN - 1)),
            dma((ZN,)),
            dma((ZN,)),
            dma((2 * ZN,)),
            dma((2 * ZN,)),
        ],
        name="moe_layer",
        compiler_params=pltpu.CompilerParams(
            collective_id=0, has_side_effects=True, vmem_limit_bytes=60 * 2**20
        ),
    )(tokens, info, w_in, m_in, v_in, g_in, w_out, m_out, v_out, g_out)
    return mixed


def per_device(tokens, routes, route_weight, w_in, m_in, v_in, g_in, w_out, m_out, v_out, g_out):
    two, depth, wide = w_in.shape[1:]
    return layer(
        tokens,
        jnp.concatenate([routes.T.astype(jnp.float32), route_weight.T], axis=0),
        *(a.reshape(two * depth, wide) for a in (w_in, m_in, v_in, g_in)),
        *(a.reshape(a.shape[1:]) for a in (w_out, m_out, v_out, g_out)),
    )


def solution(mesh):
    placed = (
        P(("dp", "expert"), None),
        P(("dp", "expert"), None),
        P(("dp", "expert"), None),
        P("expert", None, "dp", None),
        P("expert", None, "dp", None),
        P("expert", None, "dp", None),
        P("expert", None, "dp", None),
        P("expert", "dp", None),
        P("expert", "dp", None),
        P("expert", "dp", None),
        P("expert", "dp", None),
    )
    return jax.shard_map(
        per_device, mesh=mesh, in_specs=placed, out_specs=P(("dp", "expert"), None), check_vma=False
    )
```

```python
import jax
import jax.numpy as jnp
from jax import lax
from jax.experimental import pallas as pl
from jax.experimental.pallas import tpu as pltpu
from jax.sharding import PartitionSpec as P

MESH = pl.DeviceIdType.MESH
beta_one = 0.9
beta_two = 0.95
corr_one = 0.99997343860111
corr_two = 0.99407947077967
adam_eps = 1e-08
learn_rate = 0.01
weight_decay = 0.1
XN, YN, ZN = 4, 4, 4
TOPW = 4
CHUNKS = 8


def adamw(master, moment, second, gradient):
    grad_value = gradient.astype(jnp.float32)
    moment_new = beta_one * moment + (1.0 - beta_one) * grad_value
    second_new = beta_two * second + (1.0 - beta_two) * grad_value * grad_value
    update = moment_new / corr_one / (jnp.sqrt(second_new / corr_two) + adam_eps)
    return (master - learn_rate * (update + weight_decay * master)).astype(jnp.bfloat16)


def layer_kernel(
    tokens, info_in, w_in, m_in, v_in, g_in, w_out, m_out, v_out, g_out,
    mixed, tok_all,
    wi, mi, vi, gi, wo, mo, vo, go, gu_v, dn_v,
    tok, tbuf, meta, rows_v, gate_v, hid_v, res_v, ry_v, part_v, sib_v, sum_v, zin_v,
    load_sem, keep_sem, w_send, w_recv, t_send, t_recv, tin_sem, y_send, y_recv, s_send, s_recv, z_send, z_recv,
):
    d, e = lax.axis_index("dp"), lax.axis_index("expert")
    zh, x = d // XN, d % XN
    z, y, c = e // (2 * YN), e // 2 % YN, e % 2
    at_dp = lambda h, i: h * XN + lax.rem(i + XN, XN)
    right, left, far = at_dp(zh, x + 1), at_dp(zh, x - 1), at_dp(zh, x + 2)
    mirror = at_dp(1 - zh, x)
    p_right, p_left, p_far = at_dp(1 - zh, x + 1), at_dp(1 - zh, x - 1), at_dp(1 - zh, x + 2)
    at_ex = lambda zz, yy, cc: lax.rem(zz + ZN, ZN) * (2 * YN) + lax.rem(yy + YN, YN) * 2 + cc

    share_in, share_out = w_in.shape[0] // 2, w_out.shape[0]
    half, third, rest = share_in // 2, share_out // 80 * 24, share_out // 80 * 16
    pieces = [(0, 0, half), (0, half, half), (1, 0, half), (1, half, half)]
    pieces += [(2, 0, third), (2, third, third), (2, 2 * third, rest), (2, 2 * third + rest, rest)]
    tok_rows, width = tokens.shape
    load_tok = pltpu.make_async_copy(tokens, tok.at[:, pl.ds(0, width)], keep_sem.at[1])
    load_tok.start()
    loads = []
    for h, (kind, first, count) in enumerate(pieces):
        pairs = (
            ((w_in, wi), (m_in, mi), (v_in, vi), (g_in, gi))
            if kind < 2
            else ((w_out, wo), (m_out, mo), (v_out, vo), (g_out, go))
        )
        rows = pl.ds(kind * share_in + first if kind < 2 else first, count)
        loads.append(
            [pltpu.make_async_copy(a.at[rows], b.at[rows], load_sem.at[h, i]) for i, (a, b) in enumerate(pairs)]
        )
        for cp in loads[h]:
            cp.start()
    info = info_in[...]
    info_high = info.astype(jnp.bfloat16).astype(jnp.float32)
    info = jnp.concatenate(
        [info_high, info - info_high, jnp.zeros((tok_rows - 2 * info.shape[0], tok_rows), jnp.float32)], axis=0
    )
    tok[:, width:] = info.T.astype(jnp.bfloat16)

    @pl.when(z == 0)
    def _():
        zin_v[:ZN] = jnp.zeros((ZN,) + zin_v.shape[1:], zin_v.dtype)

    @pl.when(z == ZN - 1)
    def _():
        zin_v[ZN:] = jnp.zeros((ZN,) + zin_v.shape[1:], zin_v.dtype)

    barrier = pltpu.get_barrier_semaphore()
    partners = [{"dp": p, "expert": e} for p in (right, left, mirror)]
    partners += [{"dp": d, "expert": at_ex(z, y + k, c)} for k in range(1, YN)]
    partners += [{"dp": d, "expert": at_ex(z + k, y, c)} for k in range(1, ZN)]
    partners += [{"dp": d, "expert": at_ex(z, y, 1 - c)}]
    for p in partners:
        pl.semaphore_signal(barrier, inc=1, device_id=p, device_id_type=MESH)
    pl.semaphore_wait(barrier, len(partners))

    sent = []

    def tok_copy(slot, target, op, src=None):
        return pltpu.make_async_remote_copy(
            src_ref=tok_all.at[slot] if src is None else src, dst_ref=tok_all.at[slot],
            send_sem=t_send.at[op], recv_sem=t_recv.at[op],
            device_id={"dp": d, "expert": target}, device_id_type=MESH,
        )

    UP = lambda n: n - 1
    DOWN = lambda n: 2 + n
    TY = lambda b, k: 6 + b * 3 + k - 1
    TS = lambda b, k: 18 + b * 4 + k
    sibling = at_ex(z, y, 1 - c)

    def tok_spread(b, src=None):
        slot = at_ex(b, y, c)
        for k in (1, 3, 2):
            tok_copy(slot, at_ex(z, y + k, c), TY(b, k), src).start()
        tok_copy(slot, sibling, TS(b, 0), src).start()

    load_tok.wait()
    own_tok = pltpu.make_async_copy(tok, tok_all.at[e], keep_sem.at[0])
    own_tok.start()
    can_up, can_down = z < ZN - 1, z > 0

    @pl.when(can_up)
    def _():
        tok_copy(e, at_ex(z + 1, y, c), UP(1), tok).start()

    @pl.when(can_down)
    def _():
        tok_copy(e, at_ex(z - 1, y, c), DOWN(1), tok).start()

    tok_spread(z, tok)

    def tok_z(n):
        @pl.when(z >= n)
        def _():
            slot = at_ex(z - n, y, c)
            tok_copy(slot, sibling, UP(n)).wait_recv()

            if n < ZN - 1:

                @pl.when(can_up)
                def _():
                    tok_copy(slot, at_ex(z + 1, y, c), UP(n + 1)).start()

            tok_spread(z - n)

        @pl.when(z < ZN - n)
        def _():
            slot = at_ex(z + n, y, c)
            tok_copy(slot, sibling, DOWN(n)).wait_recv()

            if n < ZN - 1:

                @pl.when(can_down)
                def _():
                    tok_copy(slot, at_ex(z - 1, y, c), DOWN(n + 1)).start()

            tok_spread(z + n)

    def tok_y(n):
        def hand_on(b):
            for k in (1, 3, 2):
                slot = at_ex(b, y - k, c)
                tok_copy(slot, sibling, TY(b, k)).wait_recv()
                tok_copy(slot, sibling, TS(b, k)).start()

        if n == 0:
            hand_on(z)
            return
        pl.when(z >= n)(lambda: hand_on(z - n))
        pl.when(z < ZN - n)(lambda: hand_on(z + n))

    def tok_finish():
        for b in range(ZN):
            for k in range(1, YN):
                tok_copy(e, sibling, TY(b, k)).wait_send()
            for k in range(YN):
                tok_copy(e, sibling, TS(b, k)).wait_send()
        for n in range(1, ZN):

            @pl.when(jnp.logical_and(can_up, z >= n - 1))
            def _():
                tok_copy(e, sibling, UP(n)).wait_send()

            @pl.when(jnp.logical_and(can_down, z <= ZN - n))
            def _():
                tok_copy(e, sibling, DOWN(n)).wait_send()

    def slot_of(h, owner):
        kind, first, count = pieces[h]
        if kind < 2:
            return gu_v.at[kind, pl.ds(pl.multiple_of(owner * share_in + first, 16), count)]
        return dn_v.at[pl.ds(pl.multiple_of(owner * share_out + first, 16), count)]

    def w_copy(h, owner, target, kind):
        op = kind * CHUNKS + h
        return pltpu.make_async_remote_copy(
            src_ref=slot_of(h, owner), dst_ref=slot_of(h, owner),
            send_sem=w_send.at[op], recv_sem=w_recv.at[op],
            device_id={"dp": target, "expert": e}, device_id_type=MESH,
        )

    R_OWN, L_OWN, MIR, F_OWN, R_P, L_P, F_P = range(7)

    def w_send_to(h, owner, target, kind):
        cp = w_copy(h, owner, target, kind)
        cp.start()
        sent.append(cp)

    def w_wait(h, owner, kind):
        w_copy(h, owner, right, kind).wait_recv()

    for h in range(CHUNKS):
        for cp in loads[h]:
            cp.wait()
        kind, start, count = pieces[h]
        a, b, v, g, out = (wi, mi, vi, gi, gu_v.at[kind]) if kind < 2 else (wo, mo, vo, go, dn_v)
        first = kind * share_in + start if kind < 2 else start
        base = d * (share_in if kind < 2 else share_out) + start

        def step(i, _, a=a, b=b, v=v, g=g, out=out, first=first, base=base):
            at = pl.ds(pl.multiple_of(first + i * 16, 16), 16)
            out[pl.ds(pl.multiple_of(base + i * 16, 16), 16), :] = adamw(a[at, :], b[at, :], v[at, :], g[at, :])
            return 0

        lax.fori_loop(0, count // 16, step, 0)
        if h < 2:
            w_copy(h, d, mirror, MIR).start()
        w_send_to(h, d, right, R_OWN)
        w_send_to(h, d, left, L_OWN)

    def fwd_own(h):
        w_wait(h, left, R_OWN)
        w_wait(h, right, L_OWN)
        if h % 2 == 0:
            w_send_to(h, left, right, F_OWN)
        else:
            w_send_to(h, right, left, F_OWN)

    def to_mirror(h):
        w_copy(h - 2, d, mirror, MIR).wait_send()
        w_copy(h, d, mirror, MIR).start()

    def from_mirror(h):
        w_wait(h, mirror, MIR)
        w_send_to(h, mirror, right, R_P)
        w_send_to(h, mirror, left, L_P)

    def fwd_mirror(h):
        w_wait(h, p_left, R_P)
        w_wait(h, p_right, L_P)
        if h % 2 == 0:
            w_send_to(h, p_left, right, F_P)
        else:
            w_send_to(h, p_right, left, F_P)

    wide = dn_v.shape[0]
    blocks = tok_all.shape[0]
    cap = rows_v.shape[0] // blocks
    f32, bf16 = jnp.float32, jnp.bfloat16

    def iota(shape, dim):
        return lax.broadcasted_iota(jnp.int32, shape, dim)

    def routed(info, expert, slot):
        lanes = expert.shape[1]
        hit = jnp.zeros((tok_rows, lanes), f32)
        weight = jnp.zeros((tok_rows, lanes), f32)
        for k in range(TOPW):
            same = info[:, k : k + 1] == expert
            hit = jnp.where(same, 1.0, hit)
            share = info[:, TOPW + k : TOPW + k + 1] + info[:, 3 * TOPW + k : 3 * TOPW + k + 1]
            weight = jnp.where(same, share, weight)
        earlier = (iota((tok_rows, tok_rows), 1) < iota((tok_rows, tok_rows), 0)).astype(bf16)
        rank = jnp.dot(earlier, hit.astype(bf16), preferred_element_type=f32)
        return jnp.logical_and(rank == slot, hit > 0.0), weight

    DEEP = 4

    def tok_in(s):
        return pltpu.make_async_copy(tok_all.at[s], tbuf.at[lax.rem(s, DEEP)], tin_sem.at[lax.rem(s, DEEP)])

    def pick_rows(b):
        per = 2 * YN
        for k in range(YN):
            tok_copy(at_ex(b, y - k, 1 - c), sibling, TS(b, k)).wait_recv()
        for i in range(DEEP - 1):
            tok_in(b * per + i).start()

        def step(i, _):
            s = b * per + i

            @pl.when(i < per - DEEP + 1)
            def _():
                tok_in(s + DEEP - 1).start()

            tok_in(s).wait()
            at = lax.rem(s, DEEP)
            info = tbuf[at, :, width:]
            meta[s] = info
            ours = jnp.zeros((1, cap), f32) + e.astype(f32)
            place, _ = routed(info.astype(f32), ours, iota((1, cap), 1).astype(f32))
            picked = lax.dot_general(
                jnp.where(place, 1.0, 0.0).astype(bf16), tbuf[at, :, :width],
                (((0,), (0,)), ((), ())), preferred_element_type=f32,
            )
            rows_v[pl.ds(pl.multiple_of(s * cap, cap), cap), :] = picked.astype(bf16)
            return 0

        lax.fori_loop(0, per, step, 0)

    tall, tile = 512, 256

    def up_tiles(gated):
        def step(i, _):
            at = pl.ds(pl.multiple_of(lax.rem(i, 2) * tall, tall), tall)
            cols = pl.ds(pl.multiple_of(i // 2 * tile, tile), tile)
            product = jnp.dot(rows_v[at, :], gu_v[1 if gated else 0, :, cols], preferred_element_type=f32)
            if gated:
                hid_v[at, cols] = (jax.nn.silu(gate_v[at, cols]) * product).astype(bf16)
            else:
                gate_v[at, cols] = product
            return 0

        lax.fori_loop(0, 2 * wide // tile, step, 0)

    group = rows_v.shape[0] // ZN
    pair = 2 * cap

    def y_copy(i, zt, k, to):
        return pltpu.make_async_remote_copy(
            src_ref=res_v.at[zt, pl.ds(pl.multiple_of(to * pair, pair), pair)], dst_ref=ry_v.at[zt, pl.ds(pl.multiple_of(y * pair, pair), pair)],
            send_sem=y_send.at[i, k - 1], recv_sem=y_recv.at[i, k - 1],
            device_id={"dp": d, "expert": at_ex(z, to, c)}, device_id_type=MESH,
        )

    def down(i, zt):
        def step(n, _):
            cols = pl.ds(pl.multiple_of(n * tile, tile), tile)
            mine = pl.ds(pl.multiple_of(zt * group, group), group)
            res_v[zt, :, cols] = jnp.dot(hid_v[mine, :], dn_v[:, cols], preferred_element_type=f32).astype(bf16)
            return 0

        lax.fori_loop(0, width // tile, step, 0)
        for k in (1, 3, 2):
            y_copy(i, zt, k, lax.rem(y + k, YN)).start()
        own = pl.ds(pl.multiple_of(y * pair, pair), pair)
        ry_v[zt, own, :] = res_v[zt, own, :]

    def s_copy(i, zt):
        return pltpu.make_async_remote_copy(
            src_ref=part_v.at[zt, 1 - c], dst_ref=sib_v.at[zt], send_sem=s_send.at[i], recv_sem=s_recv.at[i],
            device_id={"dp": d, "expert": sibling}, device_id_type=MESH,
        )

    part_rows = tok_rows // 2

    def z_copy(zt, up, part):
        slot = jnp.where(up, zt, ZN + zt)
        rows = pl.ds(part * part_rows, part_rows)
        return pltpu.make_async_remote_copy(
            src_ref=sum_v.at[zt, rows], dst_ref=zin_v.at[slot, rows],
            send_sem=z_send.at[slot, part], recv_sem=z_recv.at[slot, part],
            device_id={"dp": d, "expert": at_ex(jnp.where(up, z + 1, z - 1), y, c)}, device_id_type=MESH,
        )

    def spread_rows(i, zt):
        lane = iota((1, YN * pair), 1)
        expert = (z * (2 * YN) + lane // pair * 2 + c).astype(f32)
        slot = lax.rem(lane, cap).astype(f32)
        for cc in range(2):
            place, weight = routed(meta[zt * (2 * YN) + y * 2 + cc].astype(f32), expert, slot)
            place = jnp.logical_and(place, lax.rem(lane // cap, 2) == cc)
            spread = jnp.where(place, weight, 0.0)
            high = spread.astype(bf16)
            first = cc * 2 * lane.shape[1]
            tbuf[i, :, first : first + lane.shape[1]] = high
            tbuf[i, :, first + lane.shape[1] : first + 2 * lane.shape[1]] = (spread - high.astype(f32)).astype(bf16)

    def partial(i, zt):
        for k in range(1, YN):
            y_copy(i, zt, k, y).wait_recv()
        lanes = YN * pair
        high, low = (
            jnp.concatenate([tbuf[i, :, f * lanes : (f + 1) * lanes] for f in (at, at + 2)], axis=0) for at in range(2)
        )

        def step(n, _):
            cols = pl.ds(pl.multiple_of(n * tile, tile), tile)
            arrived = ry_v[zt, :, cols]
            total = jnp.dot(high, arrived, preferred_element_type=f32) + jnp.dot(low, arrived, preferred_element_type=f32)
            part_v[zt, 0, :, cols] = total[:tok_rows].astype(bf16)
            part_v[zt, 1, :, cols] = total[tok_rows:].astype(bf16)
            return 0

        lax.fori_loop(0, width // tile, step, 0)
        s_copy(i, zt).start()

    def both_cores(i, zt, on):
        s_copy(i, zt).wait_recv()
        up = zt > z
        slot = jnp.where(up, zt, ZN + zt)
        for part in range(2):
            if on:

                @pl.when(jnp.where(up, z, ZN - 1 - z) > 0)
                def _():
                    z_copy(zt, up, part).wait_recv()

            else:
                pl.when(z > 0)(lambda: z_copy(z, True, part).wait_recv())
                pl.when(z < ZN - 1)(lambda: z_copy(z, False, part).wait_recv())

            def step(n, _):
                at = pl.ds(pl.multiple_of(part * part_rows + n * 16, 16), 16)
                total = part_v[zt, c, at, :].astype(f32) + sib_v[zt, at, :].astype(f32)
                if on:
                    sum_v[zt, at, :] = (total + zin_v[slot, at, :].astype(f32)).astype(bf16)
                else:
                    mixed[at, :] = (total + zin_v[z, at, :].astype(f32) + zin_v[ZN + z, at, :].astype(f32)).astype(bf16)
                return 0

            lax.fori_loop(0, part_rows // 16, step, 0)
            if on:
                z_copy(zt, up, part).start()

    def gate_up_arrive(*some):
        for h in some:
            w_wait(h, far, F_OWN)
            w_wait(h, p_far, F_P)

    tok_z(1)
    fwd_own(0)
    fwd_own(1)
    tok_z(2)
    fwd_own(2)
    fwd_own(3)
    from_mirror(0)
    to_mirror(2)
    tok_z(3)
    for h in range(4, CHUNKS):
        fwd_own(h)
    from_mirror(1)
    to_mirror(3)
    fwd_mirror(0)
    tok_y(0)
    tok_y(1)
    from_mirror(2)
    to_mirror(4)
    fwd_mirror(1)
    tok_y(2)
    tok_y(3)
    own_tok.wait()
    pick_rows(0)
    from_mirror(3)
    to_mirror(5)
    fwd_mirror(2)
    pick_rows(1)
    from_mirror(4)
    to_mirror(6)
    pick_rows(2)
    fwd_mirror(3)
    from_mirror(5)
    to_mirror(7)
    pick_rows(3)
    fwd_mirror(4)
    from_mirror(6)
    fwd_mirror(5)
    from_mirror(7)
    gate_up_arrive(0, 1)
    up_tiles(False)
    fwd_mirror(6)
    fwd_mirror(7)
    gate_up_arrive(2, 3)
    up_tiles(True)
    gate_up_arrive(4, 5, 6, 7)

    def by_z(*table):
        out = jnp.int32(table[-1])
        for at in range(ZN - 1):
            out = jnp.where(z == at, table[at], out)
        return out

    order = list(enumerate((by_z(3, 3, 0, 0), by_z(2, 0, 3, 1), by_z(1, 2, 1, 2), z)))
    for i, zt in order:
        down(i, zt)
    for i, zt in order:
        spread_rows(i, zt)
    for i, zt in order:
        partial(i, zt)
        both_cores(i, zt, i < ZN - 1)
    for i, zt in order:
        for k in range(1, YN):
            y_copy(i, zt, k, lax.rem(y + k, YN)).wait_send()
        s_copy(i, zt).wait_send()
        if i < ZN - 1:
            for part in range(2):
                z_copy(zt, zt > z, part).wait_send()
    for h in (CHUNKS - 2, CHUNKS - 1):
        w_copy(h, d, mirror, MIR).wait_send()
    tok_finish()
    for cp in sent:
        cp.wait_send()


def layer(tokens, info, w_in, m_in, v_in, g_in, w_out, m_out, v_out, g_out):
    rows_in, wide = w_in.shape
    rows_out, width = w_out.shape
    groups, dps = lax.axis_size("expert"), lax.axis_size("dp")
    tok_rows = tokens.shape[0]
    whole = width + 128
    cap = 2 * tok_rows * TOPW // groups
    any_space = pl.BlockSpec(memory_space=pl.ANY)
    f32, bf16 = jnp.float32, jnp.bfloat16
    dma = pltpu.SemaphoreType.DMA
    mixed, _ = pl.pallas_call(
        layer_kernel,
        out_shape=(
            jax.ShapeDtypeStruct((tok_rows, width), bf16),
            jax.ShapeDtypeStruct((groups, tok_rows, whole), bf16),
        ),
        in_specs=[any_space, pl.BlockSpec(memory_space=pltpu.VMEM)] + [any_space] * 8,
        out_specs=(pl.BlockSpec(memory_space=pltpu.VMEM), any_space),
        scratch_shapes=[pltpu.VMEM((rows_in, wide), t) for t in (f32, f32, f32, bf16)]
        + [pltpu.VMEM((rows_out, width), t) for t in (f32, f32, f32, bf16)]
        + [
            pltpu.VMEM((2, dps * rows_in // 2, wide), bf16),
            pltpu.VMEM((dps * rows_out, width), bf16),
            pltpu.VMEM((tok_rows, whole), bf16),
            pltpu.VMEM((4, tok_rows, whole), bf16),
            pltpu.VMEM((groups, tok_rows, whole - width), bf16),
            pltpu.VMEM((groups * cap, width), bf16),
            pltpu.VMEM((groups * cap, wide), f32),
            pltpu.VMEM((groups * cap, wide), bf16),
            pltpu.VMEM((ZN, groups * cap // ZN, width), bf16),
            pltpu.VMEM((ZN, 2 * YN * cap, width), bf16),
            pltpu.VMEM((ZN, 2, tok_rows, width), bf16),
            pltpu.VMEM((ZN, tok_rows, width), bf16),
            pltpu.VMEM((ZN, tok_rows, width), bf16),
            pltpu.VMEM((2 * ZN, tok_rows, width), bf16),
            dma((CHUNKS, 4)),
            dma((2,)),
            dma((7 * CHUNKS,)),
            dma((7 * CHUNKS,)),
            dma((34,)),
            dma((34,)),
            dma((4,)),
            dma((ZN, YN - 1)),
            dma((ZN, YN - 1)),
            dma((ZN,)),
            dma((ZN,)),
            dma((2 * ZN, 2)),
            dma((2 * ZN, 2)),
        ],
        name="moe_layer",
        compiler_params=pltpu.CompilerParams(
            collective_id=0, has_side_effects=True, vmem_limit_bytes=62 * 2**20
        ),
    )(tokens, info, w_in, m_in, v_in, g_in, w_out, m_out, v_out, g_out)
    return mixed


def per_device(tokens, routes, route_weight, w_in, m_in, v_in, g_in, w_out, m_out, v_out, g_out):
    two, depth, wide = w_in.shape[1:]
    return layer(
        tokens,
        jnp.concatenate([routes.T.astype(jnp.float32), route_weight.T], axis=0),
        *(a.reshape(two * depth, wide) for a in (w_in, m_in, v_in, g_in)),
        *(a.reshape(a.shape[1:]) for a in (w_out, m_out, v_out, g_out)),
    )


def solution(mesh):
    placed = (
        P(("dp", "expert"), None),
        P(("dp", "expert"), None),
        P(("dp", "expert"), None),
        P("expert", None, "dp", None),
        P("expert", None, "dp", None),
        P("expert", None, "dp", None),
        P("expert", None, "dp", None),
        P("expert", "dp", None),
        P("expert", "dp", None),
        P("expert", "dp", None),
        P("expert", "dp", None),
    )
    return jax.shard_map(
        per_device, mesh=mesh, in_specs=placed, out_specs=P(("dp", "expert"), None), check_vma=False
    )
```

```python
import jax
import jax.numpy as jnp
from jax import lax
from jax.experimental import pallas as pl
from jax.experimental.pallas import tpu as pltpu
from jax.sharding import PartitionSpec as P

MESH = pl.DeviceIdType.MESH
beta_one = 0.9
beta_two = 0.95
corr_one = 0.99997343860111
corr_two = 0.99407947077967
adam_eps = 1e-08
learn_rate = 0.01
weight_decay = 0.1
XN, YN, ZN = 4, 4, 4
TOPW = 4
CHUNKS = 8


def adamw(master, moment, second, gradient):
    grad_value = gradient.astype(jnp.float32)
    moment_new = beta_one * moment + (1.0 - beta_one) * grad_value
    second_new = beta_two * second + (1.0 - beta_two) * grad_value * grad_value
    update = moment_new / corr_one / (jnp.sqrt(second_new / corr_two) + adam_eps)
    return (master - learn_rate * (update + weight_decay * master)).astype(jnp.bfloat16)


def layer_kernel(
    tokens, info_in, w_in, m_in, v_in, g_in, w_out, m_out, v_out, g_out,
    mixed, tok_all,
    wi, mi, vi, gi, wo, mo, vo, go, gu_v, dn_v,
    tok, tbuf, meta, rows_v, gate_v, hid_v, res_v, ry_v, part_v, sib_v, sum_v, zin_v,
    load_sem, keep_sem, w_send, w_recv, t_send, t_recv, tin_sem, y_send, y_recv, s_send, s_recv, z_send, z_recv,
):
    d, e = lax.axis_index("dp"), lax.axis_index("expert")
    zh, x = d // XN, d % XN
    z, y, c = e // (2 * YN), e // 2 % YN, e % 2
    at_dp = lambda h, i: h * XN + lax.rem(i + XN, XN)
    right, left, far = at_dp(zh, x + 1), at_dp(zh, x - 1), at_dp(zh, x + 2)
    mirror = at_dp(1 - zh, x)
    p_right, p_left, p_far = at_dp(1 - zh, x + 1), at_dp(1 - zh, x - 1), at_dp(1 - zh, x + 2)
    at_ex = lambda zz, yy, cc: lax.rem(zz + ZN, ZN) * (2 * YN) + lax.rem(yy + YN, YN) * 2 + cc

    share_in, share_out = w_in.shape[0] // 2, w_out.shape[0]
    half, third, rest = share_in // 2, share_out // 80 * 24, share_out // 80 * 16
    pieces = [(0, 0, half), (0, half, half), (1, 0, half), (1, half, half)]
    pieces += [(2, 0, third), (2, third, third), (2, 2 * third, rest), (2, 2 * third + rest, rest)]
    tok_rows, width = tokens.shape
    load_tok = pltpu.make_async_copy(tokens, tok.at[:, pl.ds(0, width)], keep_sem.at[1])
    load_tok.start()
    loads = []
    for h, (kind, first, count) in enumerate(pieces):
        pairs = (
            ((w_in, wi), (m_in, mi), (v_in, vi), (g_in, gi))
            if kind < 2
            else ((w_out, wo), (m_out, mo), (v_out, vo), (g_out, go))
        )
        rows = pl.ds(kind * share_in + first if kind < 2 else first, count)
        loads.append(
            [pltpu.make_async_copy(a.at[rows], b.at[rows], load_sem.at[h, i]) for i, (a, b) in enumerate(pairs)]
        )
        for cp in loads[h]:
            cp.start()
    info = info_in[...]
    info_high = info.astype(jnp.bfloat16).astype(jnp.float32)
    info = jnp.concatenate(
        [info_high, info - info_high, jnp.zeros((tok_rows - 2 * info.shape[0], tok_rows), jnp.float32)], axis=0
    )
    tok[:, width:] = info.T.astype(jnp.bfloat16)

    @pl.when(z == 0)
    def _():
        zin_v[:ZN] = jnp.zeros((ZN,) + zin_v.shape[1:], zin_v.dtype)

    @pl.when(z == ZN - 1)
    def _():
        zin_v[ZN:] = jnp.zeros((ZN,) + zin_v.shape[1:], zin_v.dtype)

    barrier = pltpu.get_barrier_semaphore()
    partners = [{"dp": p, "expert": e} for p in (right, left, mirror)]
    partners += [{"dp": d, "expert": at_ex(z, y + k, c)} for k in range(1, YN)]
    partners += [{"dp": d, "expert": at_ex(z + k, y, c)} for k in range(1, ZN)]
    partners += [{"dp": d, "expert": at_ex(z, y, 1 - c)}]
    for p in partners:
        pl.semaphore_signal(barrier, inc=1, device_id=p, device_id_type=MESH)
    pl.semaphore_wait(barrier, len(partners))

    sent = []

    def tok_copy(slot, target, op, src=None):
        return pltpu.make_async_remote_copy(
            src_ref=tok_all.at[slot] if src is None else src, dst_ref=tok_all.at[slot],
            send_sem=t_send.at[op], recv_sem=t_recv.at[op],
            device_id={"dp": d, "expert": target}, device_id_type=MESH,
        )

    UP = lambda n: n - 1
    DOWN = lambda n: 2 + n
    TY = lambda b, k: 6 + b * 3 + k - 1
    TS = lambda b, k: 18 + b * 4 + k
    sibling = at_ex(z, y, 1 - c)

    def tok_spread(b, src=None):
        slot = at_ex(b, y, c)
        for k in (1, 3, 2):
            tok_copy(slot, at_ex(z, y + k, c), TY(b, k), src).start()
        tok_copy(slot, sibling, TS(b, 0), src).start()

    load_tok.wait()
    own_tok = pltpu.make_async_copy(tok, tok_all.at[e], keep_sem.at[0])
    own_tok.start()
    can_up, can_down = z < ZN - 1, z > 0

    @pl.when(can_up)
    def _():
        tok_copy(e, at_ex(z + 1, y, c), UP(1), tok).start()

    @pl.when(can_down)
    def _():
        tok_copy(e, at_ex(z - 1, y, c), DOWN(1), tok).start()

    tok_spread(z, tok)

    def tok_z(n):
        @pl.when(z >= n)
        def _():
            slot = at_ex(z - n, y, c)
            tok_copy(slot, sibling, UP(n)).wait_recv()

            if n < ZN - 1:

                @pl.when(can_up)
                def _():
                    tok_copy(slot, at_ex(z + 1, y, c), UP(n + 1)).start()

            tok_spread(z - n)

        @pl.when(z < ZN - n)
        def _():
            slot = at_ex(z + n, y, c)
            tok_copy(slot, sibling, DOWN(n)).wait_recv()

            if n < ZN - 1:

                @pl.when(can_down)
                def _():
                    tok_copy(slot, at_ex(z - 1, y, c), DOWN(n + 1)).start()

            tok_spread(z + n)

    def tok_y(n):
        def hand_on(b):
            for k in (1, 3, 2):
                slot = at_ex(b, y - k, c)
                tok_copy(slot, sibling, TY(b, k)).wait_recv()
                tok_copy(slot, sibling, TS(b, k)).start()

        if n == 0:
            hand_on(z)
            return
        pl.when(z >= n)(lambda: hand_on(z - n))
        pl.when(z < ZN - n)(lambda: hand_on(z + n))

    def tok_finish():
        for b in range(ZN):
            for k in range(1, YN):
                tok_copy(e, sibling, TY(b, k)).wait_send()
            for k in range(YN):
                tok_copy(e, sibling, TS(b, k)).wait_send()
        for n in range(1, ZN):

            @pl.when(jnp.logical_and(can_up, z >= n - 1))
            def _():
                tok_copy(e, sibling, UP(n)).wait_send()

            @pl.when(jnp.logical_and(can_down, z <= ZN - n))
            def _():
                tok_copy(e, sibling, DOWN(n)).wait_send()

    def slot_of(h, owner):
        kind, first, count = pieces[h]
        if kind < 2:
            return gu_v.at[kind, pl.ds(pl.multiple_of(owner * share_in + first, 16), count)]
        return dn_v.at[pl.ds(pl.multiple_of(owner * share_out + first, 16), count)]

    def w_copy(h, owner, target, kind):
        op = kind * CHUNKS + h
        return pltpu.make_async_remote_copy(
            src_ref=slot_of(h, owner), dst_ref=slot_of(h, owner),
            send_sem=w_send.at[op], recv_sem=w_recv.at[op],
            device_id={"dp": target, "expert": e}, device_id_type=MESH,
        )

    R_OWN, L_OWN, MIR, F_OWN, R_P, L_P, F_P = range(7)

    def w_send_to(h, owner, target, kind):
        cp = w_copy(h, owner, target, kind)
        cp.start()
        sent.append(cp)

    def w_wait(h, owner, kind):
        w_copy(h, owner, right, kind).wait_recv()

    for h in range(CHUNKS):
        for cp in loads[h]:
            cp.wait()
        kind, start, count = pieces[h]
        a, b, v, g, out = (wi, mi, vi, gi, gu_v.at[kind]) if kind < 2 else (wo, mo, vo, go, dn_v)
        first = kind * share_in + start if kind < 2 else start
        base = d * (share_in if kind < 2 else share_out) + start

        def step(i, _, a=a, b=b, v=v, g=g, out=out, first=first, base=base):
            at = pl.ds(pl.multiple_of(first + i * 16, 16), 16)
            out[pl.ds(pl.multiple_of(base + i * 16, 16), 16), :] = adamw(a[at, :], b[at, :], v[at, :], g[at, :])
            return 0

        lax.fori_loop(0, count // 16, step, 0)
        if h < 2:
            w_copy(h, d, mirror, MIR).start()
        w_send_to(h, d, right, R_OWN)
        w_send_to(h, d, left, L_OWN)

    def fwd_own(h):
        w_wait(h, left, R_OWN)
        w_wait(h, right, L_OWN)
        if h % 2 == 0:
            w_send_to(h, left, right, F_OWN)
        else:
            w_send_to(h, right, left, F_OWN)

    def to_mirror(h):
        w_copy(h - 2, d, mirror, MIR).wait_send()
        w_copy(h, d, mirror, MIR).start()

    def from_mirror(h):
        w_wait(h, mirror, MIR)
        w_send_to(h, mirror, right, R_P)
        w_send_to(h, mirror, left, L_P)

    def fwd_mirror(h):
        w_wait(h, p_left, R_P)
        w_wait(h, p_right, L_P)
        if h % 2 == 0:
            w_send_to(h, p_left, right, F_P)
        else:
            w_send_to(h, p_right, left, F_P)

    wide = dn_v.shape[0]
    blocks = tok_all.shape[0]
    cap = rows_v.shape[0] // blocks
    f32, bf16 = jnp.float32, jnp.bfloat16

    def iota(shape, dim):
        return lax.broadcasted_iota(jnp.int32, shape, dim)

    def routed(info, expert, slot):
        lanes = expert.shape[1]
        hit = jnp.zeros((tok_rows, lanes), f32)
        weight = jnp.zeros((tok_rows, lanes), f32)
        for k in range(TOPW):
            same = info[:, k : k + 1] == expert
            hit = jnp.where(same, 1.0, hit)
            share = info[:, TOPW + k : TOPW + k + 1] + info[:, 3 * TOPW + k : 3 * TOPW + k + 1]
            weight = jnp.where(same, share, weight)
        earlier = (iota((tok_rows, tok_rows), 1) < iota((tok_rows, tok_rows), 0)).astype(bf16)
        rank = jnp.dot(earlier, hit.astype(bf16), preferred_element_type=f32)
        return jnp.logical_and(rank == slot, hit > 0.0), weight

    DEEP = 4

    def tok_in(s):
        return pltpu.make_async_copy(tok_all.at[s], tbuf.at[lax.rem(s, DEEP)], tin_sem.at[lax.rem(s, DEEP)])

    def pick_rows(b):
        per = 2 * YN
        for k in range(YN):
            tok_copy(at_ex(b, y - k, 1 - c), sibling, TS(b, k)).wait_recv()
        for i in range(DEEP - 1):
            tok_in(b * per + i).start()

        def step(i, _):
            s = b * per + i

            @pl.when(i < per - DEEP + 1)
            def _():
                tok_in(s + DEEP - 1).start()

            tok_in(s).wait()
            at = lax.rem(s, DEEP)
            info = tbuf[at, :, width:]
            meta[s] = info
            ours = jnp.zeros((1, cap), f32) + e.astype(f32)
            place, _ = routed(info.astype(f32), ours, iota((1, cap), 1).astype(f32))
            picked = lax.dot_general(
                jnp.where(place, 1.0, 0.0).astype(bf16), tbuf[at, :, :width],
                (((0,), (0,)), ((), ())), preferred_element_type=f32,
            )
            rows_v[pl.ds(pl.multiple_of(s * cap, cap), cap), :] = picked.astype(bf16)
            return 0

        lax.fori_loop(0, per, step, 0)

    tall, tile = 512, 256

    def up_tiles(gated):
        def step(i, _):
            at = pl.ds(pl.multiple_of(lax.rem(i, 2) * tall, tall), tall)
            cols = pl.ds(pl.multiple_of(i // 2 * tile, tile), tile)
            product = jnp.dot(rows_v[at, :], gu_v[1 if gated else 0, :, cols], preferred_element_type=f32)
            if gated:
                hid_v[at, cols] = (jax.nn.silu(gate_v[at, cols]) * product).astype(bf16)
            else:
                gate_v[at, cols] = product
            return 0

        lax.fori_loop(0, 2 * wide // tile, step, 0)

    group = rows_v.shape[0] // ZN
    pair = 2 * cap

    def y_copy(i, zt, k, to):
        return pltpu.make_async_remote_copy(
            src_ref=res_v.at[zt, pl.ds(pl.multiple_of(to * pair, pair), pair)], dst_ref=ry_v.at[zt, pl.ds(pl.multiple_of(y * pair, pair), pair)],
            send_sem=y_send.at[i, k - 1], recv_sem=y_recv.at[i, k - 1],
            device_id={"dp": d, "expert": at_ex(z, to, c)}, device_id_type=MESH,
        )

    def down(i, zt):
        def step(n, _):
            cols = pl.ds(pl.multiple_of(n * tile, tile), tile)
            mine = pl.ds(pl.multiple_of(zt * group, group), group)
            res_v[zt, :, cols] = jnp.dot(hid_v[mine, :], dn_v[:, cols], preferred_element_type=f32).astype(bf16)
            return 0

        lax.fori_loop(0, width // tile, step, 0)
        for k in (1, 3, 2):
            y_copy(i, zt, k, lax.rem(y + k, YN)).start()
        own = pl.ds(pl.multiple_of(y * pair, pair), pair)
        ry_v[zt, own, :] = res_v[zt, own, :]

    def s_copy(i, zt):
        return pltpu.make_async_remote_copy(
            src_ref=part_v.at[zt, 1 - c], dst_ref=sib_v.at[zt], send_sem=s_send.at[i], recv_sem=s_recv.at[i],
            device_id={"dp": d, "expert": sibling}, device_id_type=MESH,
        )

    part_rows = tok_rows // 4

    def z_copy(zt, up, part):
        slot = jnp.where(up, zt, ZN + zt)
        rows = pl.ds(part * part_rows, part_rows)
        return pltpu.make_async_remote_copy(
            src_ref=sum_v.at[zt, rows], dst_ref=zin_v.at[slot, rows],
            send_sem=z_send.at[slot, part], recv_sem=z_recv.at[slot, part],
            device_id={"dp": d, "expert": at_ex(jnp.where(up, z + 1, z - 1), y, c)}, device_id_type=MESH,
        )

    def spread_rows(i, zt):
        lane = iota((1, YN * pair), 1)
        expert = (z * (2 * YN) + lane // pair * 2 + c).astype(f32)
        slot = lax.rem(lane, cap).astype(f32)
        for cc in range(2):
            place, weight = routed(meta[zt * (2 * YN) + y * 2 + cc].astype(f32), expert, slot)
            place = jnp.logical_and(place, lax.rem(lane // cap, 2) == cc)
            spread = jnp.where(place, weight, 0.0)
            high = spread.astype(bf16)
            first = cc * 2 * lane.shape[1]
            tbuf[i, :, first : first + lane.shape[1]] = high
            tbuf[i, :, first + lane.shape[1] : first + 2 * lane.shape[1]] = (spread - high.astype(f32)).astype(bf16)

    def partial(i, zt):
        for k in range(1, YN):
            y_copy(i, zt, k, y).wait_recv()
        lanes = YN * pair
        high, low = (
            jnp.concatenate([tbuf[i, :, f * lanes : (f + 1) * lanes] for f in (at, at + 2)], axis=0) for at in range(2)
        )

        def step(n, _):
            cols = pl.ds(pl.multiple_of(n * tile, tile), tile)
            arrived = ry_v[zt, :, cols]
            total = jnp.dot(high, arrived, preferred_element_type=f32) + jnp.dot(low, arrived, preferred_element_type=f32)
            part_v[zt, 0, :, cols] = total[:tok_rows].astype(bf16)
            part_v[zt, 1, :, cols] = total[tok_rows:].astype(bf16)
            return 0

        lax.fori_loop(0, width // tile, step, 0)
        s_copy(i, zt).start()

    def both_cores(i, zt, on):
        s_copy(i, zt).wait_recv()
        up = zt > z
        slot = jnp.where(up, zt, ZN + zt)
        for part in range(4):
            if on:

                @pl.when(jnp.where(up, z, ZN - 1 - z) > 0)
                def _():
                    z_copy(zt, up, part).wait_recv()

            else:
                pl.when(z > 0)(lambda: z_copy(z, True, part).wait_recv())
                pl.when(z < ZN - 1)(lambda: z_copy(z, False, part).wait_recv())

            def step(n, _):
                at = pl.ds(pl.multiple_of(part * part_rows + n * 16, 16), 16)
                total = part_v[zt, c, at, :].astype(f32) + sib_v[zt, at, :].astype(f32)
                if on:
                    sum_v[zt, at, :] = (total + zin_v[slot, at, :].astype(f32)).astype(bf16)
                else:
                    mixed[at, :] = (total + zin_v[z, at, :].astype(f32) + zin_v[ZN + z, at, :].astype(f32)).astype(bf16)
                return 0

            lax.fori_loop(0, part_rows // 16, step, 0)
            if on:
                z_copy(zt, up, part).start()

    def gate_up_arrive(*some):
        for h in some:
            w_wait(h, far, F_OWN)
            w_wait(h, p_far, F_P)

    tok_z(1)
    fwd_own(0)
    fwd_own(1)
    tok_z(2)
    fwd_own(2)
    fwd_own(3)
    from_mirror(0)
    to_mirror(2)
    tok_z(3)
    for h in range(4, CHUNKS):
        fwd_own(h)
    from_mirror(1)
    to_mirror(3)
    fwd_mirror(0)
    tok_y(0)
    tok_y(1)
    from_mirror(2)
    to_mirror(4)
    fwd_mirror(1)
    tok_y(2)
    tok_y(3)
    own_tok.wait()
    pick_rows(0)
    from_mirror(3)
    to_mirror(5)
    fwd_mirror(2)
    pick_rows(1)
    from_mirror(4)
    to_mirror(6)
    pick_rows(2)
    fwd_mirror(3)
    from_mirror(5)
    to_mirror(7)
    pick_rows(3)
    fwd_mirror(4)
    from_mirror(6)
    fwd_mirror(5)
    from_mirror(7)
    gate_up_arrive(0, 1)
    up_tiles(False)
    fwd_mirror(6)
    fwd_mirror(7)
    gate_up_arrive(2, 3)
    up_tiles(True)
    gate_up_arrive(4, 5, 6, 7)

    def by_z(*table):
        out = jnp.int32(table[-1])
        for at in range(ZN - 1):
            out = jnp.where(z == at, table[at], out)
        return out

    order = list(enumerate((by_z(3, 3, 0, 0), by_z(2, 0, 3, 1), by_z(1, 2, 1, 2), z)))
    for i, zt in order:
        down(i, zt)
    for i, zt in order:
        spread_rows(i, zt)
    for i, zt in order:
        partial(i, zt)
        both_cores(i, zt, i < ZN - 1)
    for i, zt in order:
        for k in range(1, YN):
            y_copy(i, zt, k, lax.rem(y + k, YN)).wait_send()
        s_copy(i, zt).wait_send()
        if i < ZN - 1:
            for part in range(4):
                z_copy(zt, zt > z, part).wait_send()
    for h in (CHUNKS - 2, CHUNKS - 1):
        w_copy(h, d, mirror, MIR).wait_send()
    tok_finish()
    for cp in sent:
        cp.wait_send()


def layer(tokens, info, w_in, m_in, v_in, g_in, w_out, m_out, v_out, g_out):
    rows_in, wide = w_in.shape
    rows_out, width = w_out.shape
    groups, dps = lax.axis_size("expert"), lax.axis_size("dp")
    tok_rows = tokens.shape[0]
    whole = width + 128
    cap = 2 * tok_rows * TOPW // groups
    any_space = pl.BlockSpec(memory_space=pl.ANY)
    f32, bf16 = jnp.float32, jnp.bfloat16
    dma = pltpu.SemaphoreType.DMA
    mixed, _ = pl.pallas_call(
        layer_kernel,
        out_shape=(
            jax.ShapeDtypeStruct((tok_rows, width), bf16),
            jax.ShapeDtypeStruct((groups, tok_rows, whole), bf16),
        ),
        in_specs=[any_space, pl.BlockSpec(memory_space=pltpu.VMEM)] + [any_space] * 8,
        out_specs=(pl.BlockSpec(memory_space=pltpu.VMEM), any_space),
        scratch_shapes=[pltpu.VMEM((rows_in, wide), t) for t in (f32, f32, f32, bf16)]
        + [pltpu.VMEM((rows_out, width), t) for t in (f32, f32, f32, bf16)]
        + [
            pltpu.VMEM((2, dps * rows_in // 2, wide), bf16),
            pltpu.VMEM((dps * rows_out, width), bf16),
            pltpu.VMEM((tok_rows, whole), bf16),
            pltpu.VMEM((4, tok_rows, whole), bf16),
            pltpu.VMEM((groups, tok_rows, whole - width), bf16),
            pltpu.VMEM((groups * cap, width), bf16),
            pltpu.VMEM((groups * cap, wide), f32),
            pltpu.VMEM((groups * cap, wide), bf16),
            pltpu.VMEM((ZN, groups * cap // ZN, width), bf16),
            pltpu.VMEM((ZN, 2 * YN * cap, width), bf16),
            pltpu.VMEM((ZN, 2, tok_rows, width), bf16),
            pltpu.VMEM((ZN, tok_rows, width), bf16),
            pltpu.VMEM((ZN, tok_rows, width), bf16),
            pltpu.VMEM((2 * ZN, tok_rows, width), bf16),
            dma((CHUNKS, 4)),
            dma((2,)),
            dma((7 * CHUNKS,)),
            dma((7 * CHUNKS,)),
            dma((34,)),
            dma((34,)),
            dma((4,)),
            dma((ZN, YN - 1)),
            dma((ZN, YN - 1)),
            dma((ZN,)),
            dma((ZN,)),
            dma((2 * ZN, 4)),
            dma((2 * ZN, 4)),
        ],
        name="moe_layer",
        compiler_params=pltpu.CompilerParams(
            collective_id=0, has_side_effects=True, vmem_limit_bytes=62 * 2**20
        ),
    )(tokens, info, w_in, m_in, v_in, g_in, w_out, m_out, v_out, g_out)
    return mixed


def per_device(tokens, routes, route_weight, w_in, m_in, v_in, g_in, w_out, m_out, v_out, g_out):
    two, depth, wide = w_in.shape[1:]
    return layer(
        tokens,
        jnp.concatenate([routes.T.astype(jnp.float32), route_weight.T], axis=0),
        *(a.reshape(two * depth, wide) for a in (w_in, m_in, v_in, g_in)),
        *(a.reshape(a.shape[1:]) for a in (w_out, m_out, v_out, g_out)),
    )


def solution(mesh):
    placed = (
        P(("dp", "expert"), None),
        P(("dp", "expert"), None),
        P(("dp", "expert"), None),
        P("expert", None, "dp", None),
        P("expert", None, "dp", None),
        P("expert", None, "dp", None),
        P("expert", None, "dp", None),
        P("expert", "dp", None),
        P("expert", "dp", None),
        P("expert", "dp", None),
        P("expert", "dp", None),
    )
    return jax.shard_map(
        per_device, mesh=mesh, in_specs=placed, out_specs=P(("dp", "expert"), None), check_vma=False
    )
```
